256 devices in a mesh: seq: 8 (over x, z_hi), res: 32 (over z_lo, y, core).
Axes of the slice: x: 4, y: 4, z: 8 (z_hi: 2, z_lo: 4; z = z_hi * 4 + z_lo), core: 2. Of those that a mesh axis runs over, the one named last changes fastest.
Arguments:
- extra_activations: bfloat16 [256, 65536], P('seq', 'res'), may hold values from -6 to 6
- twofold_representation: bfloat16 [1024, 1024, 128], P('res', 'seq'), may hold values from -6 to 6
- present_indicator: int32 [256, 1024], P('seq', 'res'), may hold values 0 or 1
- amino_presence: int32 [1024], P('res'), may hold values 0 or 1
- twofold_offset_matrix: bfloat16 [128, 8], replicated, may hold values from -1.5859375 to 1.5859375
- horizontal_matrix: bfloat16 [64, 256], replicated, may hold values from -8 to 8, as said below
- horizontal_exit_matrix: bfloat16 [64, 64], replicated, may hold values from -1.5 to 1.5
- vertical_matrix: bfloat16 [64, 144], replicated, may hold values from -8 to 8, as said below
- vertical_exit_matrix: bfloat16 [64, 64], replicated, may hold values from -0.75 to 0.75
Outputs:
- msa_out: bfloat16 [256, 65536], P('seq', 'res')
The draws below stay inside these ranges and needn't reach their ends.
Inputs may be any that keep to these rules, and one draw needn't show every extreme that they name: `horizontal_matrix`: a projection matrix. `vertical_matrix`: a projection matrix.
All inputs are finite; a program needn't handle non-finite values. No bound on the sum of `present_indicator` or of `amino_presence` on one device may be relied on, other than what follows from the above.
Results may differ from the reference program's by a relative error of at most 0.02.
The reference program's roundings to bfloat16 on the way count: a program that leaves them out, or rounds other values in their place, can miss the bound.
Values may be sent and summed in bfloat16 or wider, within the bound.
A program may use at most 64 MiB of HBM per device.

```python
import jax
import jax.numpy as jnp
from jax import lax

EXTRA_FEATURES = 64
CZ = 128
ATTN_HEAD_SUM = 8
PER_HEAD_FEATURE = 8
HOMOLOG_SUM = 256
AMINO_ACID_SUM = 1024


def draw_extra_activations(key, part):
    key = jax.random.fold_in(key, 37)
    random_first = jax.random.fold_in(key, 0)
    random_draws = jax.random.normal(random_first, (HOMOLOG_SUM, AMINO_ACID_SUM, EXTRA_FEATURES), jnp.float32)
    answer_tuple = random_draws
    answer_tuple = jnp.clip(answer_tuple, -6.0, 6.0)
    return answer_tuple.reshape(HOMOLOG_SUM, AMINO_ACID_SUM * EXTRA_FEATURES).astype(jnp.bfloat16)


def draw_horizontal_matrix(key, part):
    key = jax.random.fold_in(key, 11)
    random_first, random_second = jax.random.split(key)
    hidden_size = ATTN_HEAD_SUM * PER_HEAD_FEATURE
    broadcast_factor = jax.random.normal(random_first, (EXTRA_FEATURES, hidden_size), jnp.float32) * EXTRA_FEATURES ** (-0.5)
    remainder_list = jax.random.normal(random_second, (EXTRA_FEATURES, 3 * hidden_size), jnp.float32) * EXTRA_FEATURES ** (-0.5)
    queries = broadcast_factor
    keyed = remainder_list[:, :hidden_size]
    answer_tuple = jnp.concatenate([queries, keyed, remainder_list[:, hidden_size:]], axis=1)
    return answer_tuple.astype(jnp.bfloat16)


def draw_vertical_matrix(key, part):
    key = jax.random.fold_in(key, 23)
    random_second = jax.random.fold_in(key, 1)
    random_third = jax.random.fold_in(key, 2)
    hidden_size = ATTN_HEAD_SUM * PER_HEAD_FEATURE
    remainder_list = jax.random.normal(random_second, (EXTRA_FEATURES, 2 * hidden_size), jnp.float32) * EXTRA_FEATURES ** (-0.5)
    trailing_part = jax.random.normal(random_third, (EXTRA_FEATURES, 2 * PER_HEAD_FEATURE), jnp.float32) * EXTRA_FEATURES ** (-0.5)
    queries = remainder_list[:, :hidden_size]
    keyed = trailing_part[:, :PER_HEAD_FEATURE]
    answer_tuple = jnp.concatenate([queries, remainder_list[:, hidden_size:], keyed, trailing_part[:, PER_HEAD_FEATURE:]], axis=1)
    return answer_tuple.astype(jnp.bfloat16)


def touch_ends(result, rng, low, top_value):
    longest = result.shape.index(max(result.shape))
    spots = []
    for shift in (0, 1):
        where = [jax.random.randint(jax.random.fold_in(rng, axis), (), 0, length) for axis, length in enumerate(result.shape)]
        where[longest] = (where[longest] + shift) % result.shape[longest]
        spots.append(tuple(where))
    return result.at[spots[0]].set(low).at[spots[1]].set(top_value)


def shard_levels(stream_key, extent, shards, smallest, top_value):
    level, own = 1.0, jax.random.fold_in(stream_key, 6)
    for position, blocks in shards:
        draws = jnp.exp(jax.random.uniform(jax.random.fold_in(own, position), (blocks,), jnp.float32, smallest / len(shards), top_value / len(shards)))
        level = level * jnp.repeat(draws, extent[position] // blocks).reshape([-1 if axis == position else 1 for axis in range(len(extent))])
    return level


def noise(stream_key, shape, width, limit, cuts=(), kind=jnp.bfloat16):
    entries = jax.random.normal(stream_key, shape, jnp.float32) * width
    if len(cuts) > 0:
        entries = shard_levels(stream_key, shape, cuts, -0.22, 0.18) * entries
    return jnp.clip(entries, min=-limit, max=limit).astype(kind)


def setup_inputs(seed: int = 0) -> dict:
    keys = jax.random.split(jax.random.key(seed), 10)
    extra_activations = draw_extra_activations(jax.random.fold_in(keys[9], 71), 0)
    twofold_representation = noise(keys[1], (AMINO_ACID_SUM, AMINO_ACID_SUM, CZ), 1.0, 6.0, ((0, 32), (1, 8)))
    present_indicator = touch_ends((jax.random.randint(keys[2], (HOMOLOG_SUM, AMINO_ACID_SUM), 0, 20) < 17).astype(jnp.int32), jax.random.fold_in(keys[2], 1), 0, 1)
    amino_presence = touch_ends((jax.random.randint(keys[3], (AMINO_ACID_SUM,), 0, 10) < 9).astype(jnp.int32), jax.random.fold_in(keys[3], 1), 0, 1)
    twofold_offset_matrix = noise(keys[4], (CZ, ATTN_HEAD_SUM), (3 * CZ ** -0.5), 1.5859375)
    horizontal_matrix = draw_horizontal_matrix(jax.random.fold_in(keys[9], 71), 0)
    horizontal_exit_matrix = noise(keys[6], (ATTN_HEAD_SUM * PER_HEAD_FEATURE, EXTRA_FEATURES), (2 * (ATTN_HEAD_SUM * PER_HEAD_FEATURE) ** -0.5), 1.5)
    vertical_matrix = draw_vertical_matrix(jax.random.fold_in(keys[9], 71), 0)
    vertical_exit_matrix = noise(keys[8], (ATTN_HEAD_SUM * PER_HEAD_FEATURE, EXTRA_FEATURES), (ATTN_HEAD_SUM * PER_HEAD_FEATURE) ** -0.5, 0.75)
    return dict(extra_activations=extra_activations, twofold_representation=twofold_representation, present_indicator=present_indicator, amino_presence=amino_presence, twofold_offset_matrix=twofold_offset_matrix, horizontal_matrix=horizontal_matrix, horizontal_exit_matrix=horizontal_exit_matrix, vertical_matrix=vertical_matrix, vertical_exit_matrix=vertical_exit_matrix)


def layer_normalize(values_in):
    centre = values_in - lax.optimization_barrier(jnp.mean(values_in, axis=-1, keepdims=True))
    spread = lax.optimization_barrier(jnp.mean(centre * centre, axis=-1, keepdims=True))
    return centre * lax.rsqrt(spread + 1e-05)

def column_delta(homolog_line, kept_entries, vertical_matrix, vertical_exit_matrix, head_number, head_channel_width):
    sequence_count, column_count, feature_size = homolog_line.shape
    hidden_size = head_number * head_channel_width
    column_normalized = layer_normalize(homolog_line.astype(jnp.float32)).astype(jnp.bfloat16)
    mapped_linear = jnp.dot(column_normalized.reshape(-1, feature_size), vertical_matrix, preferred_element_type=jnp.float32)
    mapped_linear = mapped_linear.reshape(sequence_count, column_count, -1)
    column_query = mapped_linear[..., :hidden_size]
    column_gate = mapped_linear[..., hidden_size:2 * hidden_size]
    column_key = mapped_linear[..., 2 * hidden_size:2 * hidden_size + head_channel_width]
    column_value = mapped_linear[..., 2 * hidden_size + head_channel_width:]
    query_total = lax.optimization_barrier(jnp.sum(kept_entries[..., None] * column_query, axis=0))
    kept_count = lax.optimization_barrier(jnp.sum(kept_entries, axis=0))
    mean_query = query_total / jnp.maximum(kept_count, 1.0)[:, None] * head_channel_width ** (-0.5)
    logits = jnp.einsum('ihc,sic->sih', mean_query.reshape(column_count, head_number, head_channel_width), column_key)
    logits = logits + 1000000000.0 * (kept_entries - 1.0)[..., None]
    exped = jnp.exp(logits - lax.optimization_barrier(jnp.max(logits, axis=0, keepdims=True)))
    attended_output = jnp.einsum('sih,sic->ihc', exped, column_value) / lax.optimization_barrier(jnp.sum(exped, axis=0))[..., None]
    gated = jax.nn.sigmoid(column_gate).reshape(sequence_count, column_count, head_number, head_channel_width) * attended_output[None]
    gated = gated.reshape(sequence_count * column_count, hidden_size).astype(jnp.bfloat16)
    horizontal_update = jnp.dot(gated, vertical_exit_matrix, preferred_element_type=jnp.float32).reshape(sequence_count, column_count, feature_size)
    return (homolog_line.astype(jnp.float32) + horizontal_update).astype(jnp.bfloat16)

def reference(extra_activations, twofold_representation, present_indicator, amino_presence, twofold_offset_matrix, horizontal_matrix, horizontal_exit_matrix, vertical_matrix, vertical_exit_matrix):
    hidden_size = ATTN_HEAD_SUM * PER_HEAD_FEATURE
    horizontal_items = extra_activations.reshape(HOMOLOG_SUM, AMINO_ACID_SUM, EXTRA_FEATURES)
    kept_entries = (present_indicator * amino_presence[None, :]).astype(jnp.float32)
    standardised = layer_normalize(horizontal_items.astype(jnp.float32)).astype(jnp.bfloat16)
    mapped_linear = jnp.dot(standardised.reshape(-1, EXTRA_FEATURES), horizontal_matrix, preferred_element_type=jnp.float32)
    mapped_linear = mapped_linear.reshape(HOMOLOG_SUM, AMINO_ACID_SUM, 4 * hidden_size)
    queries = (mapped_linear[..., :hidden_size] * PER_HEAD_FEATURE ** (-0.5)).astype(jnp.bfloat16)
    keys_all = mapped_linear[..., hidden_size:2 * hidden_size].astype(jnp.bfloat16)
    values_all = mapped_linear[..., 2 * hidden_size:3 * hidden_size].astype(jnp.bfloat16)
    gating = mapped_linear[..., 3 * hidden_size:]
    pair_normed = layer_normalize(twofold_representation.astype(jnp.float32)).astype(jnp.bfloat16)
    pair_bias = jnp.dot(pair_normed.reshape(-1, CZ), twofold_offset_matrix, preferred_element_type=jnp.float32)
    pair_bias = pair_bias.reshape(AMINO_ACID_SUM, AMINO_ACID_SUM, ATTN_HEAD_SUM).astype(jnp.bfloat16)
    bias_heads = jnp.transpose(pair_bias.astype(jnp.float32), (2, 0, 1))

    def one_row(inputs):
        row_query, row_key, row_value, row_kept = inputs
        query_heads = row_query.astype(jnp.float32).reshape(AMINO_ACID_SUM, ATTN_HEAD_SUM, PER_HEAD_FEATURE)
        key_heads = row_key.astype(jnp.float32).reshape(AMINO_ACID_SUM, ATTN_HEAD_SUM, PER_HEAD_FEATURE)
        value_heads = row_value.astype(jnp.float32).reshape(AMINO_ACID_SUM, ATTN_HEAD_SUM, PER_HEAD_FEATURE)
        logits = jnp.einsum('ihc,jhc->hij', query_heads, key_heads) + bias_heads
        logits = logits + 1000000000.0 * (row_kept - 1.0)[None, None, :]
        exped = jnp.exp(logits - lax.optimization_barrier(jnp.max(logits, axis=-1, keepdims=True)))
        weights = exped.astype(jnp.bfloat16).astype(jnp.float32)
        summed = jnp.einsum('hij,jhc->ihc', weights, value_heads)
        summed = summed / jnp.transpose(lax.optimization_barrier(jnp.sum(exped, axis=-1)), (1, 0))[..., None]
        return summed.reshape(AMINO_ACID_SUM, hidden_size)
    attended_output = lax.map(one_row, (queries, keys_all, values_all, kept_entries))
    row_gated = (jax.nn.sigmoid(gating) * attended_output).astype(jnp.bfloat16)
    horizontal_update = jnp.dot(row_gated.reshape(-1, hidden_size), horizontal_exit_matrix, preferred_element_type=jnp.float32)
    homolog_line = (horizontal_items.astype(jnp.float32) + horizontal_update.reshape(HOMOLOG_SUM, AMINO_ACID_SUM, EXTRA_FEATURES)).astype(jnp.bfloat16)
    ultimate_update = column_delta(homolog_line, kept_entries, vertical_matrix, vertical_exit_matrix, ATTN_HEAD_SUM, PER_HEAD_FEATURE)
    return ultimate_update.reshape(HOMOLOG_SUM, AMINO_ACID_SUM * EXTRA_FEATURES)
```

```python
import jax
import jax.numpy as jnp
from jax import lax
from jax.experimental import pallas as pl
from jax.experimental.pallas import tpu as pltpu
from jax.sharding import PartitionSpec as P

MESH = pl.DeviceIdType.MESH
F32, BF16 = jnp.float32, jnp.bfloat16
SEQS, RES, PAIRS, LANES = 32, 32, 16, 128
ROWS = PAIRS + SEQS * PAIRS
GROUPS = 4
LOG2E = 1.4426950408889634
SPANS = [
    (0 if g == 0 else PAIRS + g * 128, 128 + (PAIRS if g == 0 else 0)) for g in range(GROUPS)
]


def rows_of(shape):
    return lax.broadcasted_iota(jnp.int32, shape, 0)


def lanes_of(shape):
    return lax.broadcasted_iota(jnp.int32, shape, 1)


def flag(condition):
    return jnp.where(condition, 1.0, 0.0).astype(BF16)


def dot(left, right):
    return jnp.dot(left, right, preferred_element_type=F32)


def dot_nt(left, right):
    return lax.dot_general(left, right, (((1,), (1,)), ((), ())), preferred_element_type=F32)


def dot_split(left, right):
    high = left.astype(BF16)
    low = (left - high.astype(F32)).astype(BF16)
    return dot(high, right) + dot(low, right)


def normalize(values, width):
    shape = (LANES, LANES)
    average = jnp.where(
        rows_of(shape) // width == lanes_of(shape) // width, 1.0 / width, 0.0
    ).astype(BF16)
    centre = values.astype(F32) - dot(values, average)
    spread = dot_split(centre * centre, average)
    return centre * lax.rsqrt(spread + 1e-05)


def tile_rows(weights, shift):
    height, width = weights.shape
    tall = dot(flag(rows_of((LANES, height)) % height == lanes_of((LANES, height))), weights)
    column = rows_of((width, LANES))
    pick = flag(column == lanes_of((width, LANES)) % 64 + shift)
    return dot(tall.astype(BF16), pick)


def twice(weights, shift):
    shape = (LANES, LANES)
    return jnp.where(
        rows_of(shape) // 64 == lanes_of(shape) // 64, tile_rows(weights, shift), 0.0
    ).astype(BF16)


def gather_kernel(
    x_ref,
    pair_ref,
    present_ref,
    amino_ref,
    offset_ref,
    blocks_ref,
    biases_ref,
    lines,
    offsets,
    send_sem,
    recv_sem,
    bias_send,
    bias_recv,
):
    seq, res = lax.axis_index("seq"), lax.axis_index("res")
    core, y, z = res % 2, (res // 2) % 4, res // 8
    up, down, across = (y + 1) % 4, (y + 3) % 4, (y + 2) % 4

    def place(z_at, y_at, core_at):
        return (z_at * 4 + y_at) * 2 + core_at

    seq_peers = [seq // 2 * 2 + (1 - seq % 2)] + [(seq + 2 * d) % 8 for d in (1, 2, 3)]
    res_peers = [place((z + d) % 4, y, core) for d in (1, 2, 3)]
    res_peers += [place(z, up, core), place(z, down, core), place(z, y, 1 - core)]
    barrier = pltpu.get_barrier_semaphore()
    for peer in seq_peers:
        pl.semaphore_signal(barrier, inc=1, device_id=(peer, res), device_id_type=MESH)
    for peer in res_peers:
        pl.semaphore_signal(barrier, inc=1, device_id=(seq, peer), device_id_type=MESH)

    for tile in range(PAIRS):
        lines[:, tile, :] = x_ref[:, tile * LANES : (tile + 1) * LANES].astype(F32)
    values = lines[...].reshape(SEQS * PAIRS, LANES).astype(BF16)
    blocks_ref[res, PAIRS:ROWS, :] = normalize(values, 64).astype(BF16)
    kept = (present_ref[...] * amino_ref[...]).astype(F32).astype(BF16)
    turned = jnp.zeros((PAIRS, LANES), F32)
    for parity in range(2):
        shape = (PAIRS, SEQS)
        picked = dot_nt(flag(lanes_of(shape) == 2 * rows_of(shape) + parity), kept)
        shape = (SEQS, LANES)
        turned += dot(
            picked.astype(BF16), flag(lanes_of(shape) == rows_of(shape) + parity * SEQS)
        )
    blocks_ref[res, 0:PAIRS, :] = jnp.where(
        lanes_of((PAIRS, LANES)) < 64, 1000000000.0 * (turned - 1.0), 1.0
    ).astype(BF16)

    pl.semaphore_wait(barrier, len(seq_peers) + len(res_peers))

    def chunk(block, group):
        start, size = SPANS[group]
        return blocks_ref.at[block, pl.ds(start, size), :]

    def copy(block, group, slot, target):
        return pltpu.make_async_remote_copy(
            src_ref=chunk(block, group),
            dst_ref=chunk(block, group),
            send_sem=send_sem.at[group, slot],
            recv_sem=recv_sem.at[block, group],
            device_id=(seq, target),
            device_id_type=MESH,
        )

    def arrived(block, group):
        copy(block, group, 0, res).wait_recv()

    sent = []

    def send(block, group, slot, target):
        copy(block, group, slot, target).start()

    for group in range(GROUPS):
        for d in (1, 2, 3):
            send(res, group, d - 1, res_peers[d - 1])

    shape = (8, 8)
    offset_turned = dot_nt(flag(rows_of(shape) == lanes_of(shape)), offset_ref[...]).astype(BF16)

    def bias_rows(step, carry):
        pair = pair_ref[pl.ds(step * 4, 4)].reshape(4 * LANES, LANES)
        normed = normalize(pair, LANES).astype(BF16)
        found = dot_nt(offset_turned, normed)
        for row in range(4):
            offsets[pl.ds(pl.multiple_of(step * 32 + row * 8, 8), 8), :] = found[
                :, row * LANES : (row + 1) * LANES
            ]
        return carry

    lax.fori_loop(0, 8, bias_rows, 0)
    for head in range(8):
        for parity in range(2):
            biases_ref[seq, pl.ds(head * 32 + parity * 16, 16), :] = offsets[
                pl.ds(parity * 8 + head, 16, stride=16), :
            ].astype(BF16)

    def bias_copy(block, slot, target):
        return pltpu.make_async_remote_copy(
            src_ref=biases_ref.at[block],
            dst_ref=biases_ref.at[block],
            send_sem=bias_send.at[slot],
            recv_sem=bias_recv.at[block],
            device_id=(target, res),
            device_id_type=MESH,
        )

    for slot, peer in enumerate(seq_peers):
        bias_copy(seq, slot, peer).start()

    def stage_near(group):
        for at in range(4):
            block = place(at, y, core)

            @pl.when(z != at)
            def _():
                arrived(block, group)

            send(block, group, 3 + at, res_peers[3])
            send(block, group, 7 + at, res_peers[4])
            send(block, group, 11 + at, res_peers[5])

    def stage_next(group):
        for at in range(4):
            low, high = place(at, down, core), place(at, up, core)
            arrived(low, group)
            if at % 2 == 0:
                send(low, group, 15 + at, res_peers[3])
            send(low, group, 19 + at, res_peers[5])
            arrived(high, group)
            if at % 2 == 1:
                send(high, group, 15 + at, res_peers[4])
            send(high, group, 23 + at, res_peers[5])

    def stage_far(group):
        for at in range(4):
            far = place(at, across, core)
            arrived(far, group)
            send(far, group, 27 + at, res_peers[5])

    def stage_core(group):
        for at in range(4):
            for row in range(4):
                arrived(place(at, row, 1 - core), group)

    partner = seq_peers[0]
    for step in range(GROUPS + 3):
        if step < GROUPS:
            stage_near(step)
        if step == 0:
            bias_copy(partner, 0, seq).wait_recv()
            for slot, peer in enumerate(seq_peers[1:]):
                bias_copy(partner, 4 + slot, peer).start()
        if 0 <= step - 1 < GROUPS:
            stage_next(step - 1)
        if 0 <= step - 2 < GROUPS:
            stage_far(step - 2)
        if 0 <= step - 3 < GROUPS:
            stage_core(step - 3)
    for peer in seq_peers[1:]:
        bias_copy(peer, 0, seq).wait_recv()
        bias_copy(peer // 2 * 2 + (1 - peer % 2), 0, seq).wait_recv()
    for slot in range(7):
        bias_copy(seq, slot, seq).wait_send()
    for group in range(GROUPS):
        for slot in range(31):
            copy(res, group, slot, res).wait_send()


def attend_kernel(
    blocks_ref, biases_ref, weights_ref, gated_ref, bias, queries, gates
):
    res = lax.axis_index("res")
    own = blocks_ref[res, PAIRS:ROWS, :]
    weights = weights_ref[...]
    square = (LANES, LANES)
    row, lane = rows_of(square), lanes_of(square)

    wide = (LANES, 256)
    turned = dot_nt(flag(lanes_of(wide) == rows_of(wide) % 64 + 64), weights).astype(BF16)
    across = (64, LANES)
    turned = dot(turned, flag(rows_of(across) == lanes_of(across) % 64))
    query_weights = tile_rows(weights, 0)
    gate_weights = tile_rows(weights, 192)
    for side in range(2):
        mine = row // 64 == side
        query = dot(own, jnp.where(mine, query_weights, 0.0).astype(BF16))
        query = (query * (LOG2E * 8**-0.5)).astype(BF16)
        gate = dot(own, jnp.where(mine, gate_weights, 0.0).astype(BF16))
        gates[:, side * 16 : side * 16 + 16, :] = jax.nn.sigmoid(gate).reshape(
            SEQS, PAIRS, LANES
        )
        for head in range(8):
            keyed = jnp.where(row // 8 == head, turned, 0.0)
            both = jnp.concatenate(
                [jnp.where(lane // 64 == parity, keyed, 0.0) for parity in range(2)], axis=1
            ).astype(BF16)
            found = dot(query, both).astype(BF16)
            for parity in range(2):
                start = (parity * 8 + head) * 32 + side * 16
                queries[:, start : start + 16, :] = found[
                    :, parity * LANES : (parity + 1) * LANES
                ].reshape(SEQS, PAIRS, LANES)

    shape = (256, 256)
    order = flag(rows_of(shape) == 2 * (lanes_of(shape) % LANES) + lanes_of(shape) // LANES)
    for tile in range(4):
        both = jnp.concatenate([biases_ref[2 * tile], biases_ref[2 * tile + 1]], axis=1)
        placed = dot(both, order) * LOG2E
        for parity in range(2):
            bias[parity * 256 : parity * 256 + 256, tile * LANES : (tile + 1) * LANES] = placed[
                :, parity * LANES : (parity + 1) * LANES
            ]

    value_weights = jnp.where(lane >= 64, tile_rows(weights, 128), 0.0).astype(BF16)
    mask = blocks_ref[:, 0:PAIRS, :].reshape(512, LANES)
    half = lanes_of((256, LANES)) < 64
    head_of = lanes_of((32, LANES)) // 8 - 8

    def one_line(line, carry):
        start = pl.multiple_of(PAIRS + line * PAIRS, PAIRS)
        keys = blocks_ref[:, pl.ds(start, PAIRS), :].reshape(512, LANES)
        right = jnp.concatenate([keys, mask], axis=1)
        tall = (512, LANES)
        picks = flag(lanes_of(tall) == rows_of(tall) // 256 * SEQS + line)
        left = jnp.concatenate([queries[line], picks], axis=1)
        logits = dot_nt(left, right) + bias[...]
        peak = jnp.max(logits, axis=1, keepdims=True)
        peak = jnp.maximum(peak[:256], peak[256:])
        exped = jnp.exp2(logits - jnp.concatenate([peak, peak], axis=0)).astype(BF16)
        summed = dot(exped, right)
        taken = jnp.where(half, summed[:256, :LANES], summed[256:, :LANES]).astype(BF16)
        total = summed[:256, LANES:] + summed[256:, LANES:]
        found = dot(taken, value_weights) / total
        attended = jnp.zeros((32, LANES), F32)
        for head in range(8):
            attended = jnp.where(head_of == head, found[head * 32 : head * 32 + 32], attended)
        gated_ref[line] = (gates[line] * attended).astype(BF16)
        return carry

    lax.fori_loop(0, SEQS, one_line, 0)


def column_kernel(
    x_ref,
    gated_ref,
    present_ref,
    amino_ref,
    exit_ref,
    weights_ref,
    exit_col_ref,
    out_ref,
    lines,
    results,
    means,
    sums,
    mean_send,
    mean_recv,
    sum_send,
    sum_recv,
):
    seq, res = lax.axis_index("seq"), lax.axis_index("res")
    peers = [(seq + d) % 8 for d in range(1, 8)]
    barrier = pltpu.get_barrier_semaphore()
    for peer in peers:
        pl.semaphore_signal(barrier, inc=1, device_id=(peer, res), device_id_type=MESH)

    for tile in range(PAIRS):
        lines[:, tile, :] = x_ref[:, tile * LANES : (tile + 1) * LANES].astype(F32)
    spread = (RES, RES * 64)
    kept = (present_ref[...] * amino_ref[...]).astype(F32).astype(BF16)
    kept = dot(kept, flag(rows_of(spread) == lanes_of(spread) // 64))
    for tile in range(PAIRS):
        results[:, tile, :] = kept[:, tile * LANES : (tile + 1) * LANES]
    kept = results[...]

    square = (LANES, LANES)
    row, lane = rows_of(square), lanes_of(square)
    exits = tile_rows(exit_ref[...], 0)
    update = jnp.zeros((SEQS * PAIRS, LANES), F32)
    for side in range(2):
        exit_side = jnp.where((row >= 64) & (lane // 64 == side), exits, 0.0).astype(BF16)
        gated = gated_ref[:, side * 16 : side * 16 + 16, :].reshape(SEQS * PAIRS, LANES)
        update += dot(gated, exit_side)
    whole = (SEQS, PAIRS, LANES)
    flat = (SEQS * PAIRS, LANES)
    line = (lines[...].reshape(flat) + update).astype(BF16)
    normed = normalize(line, 64).astype(BF16)

    pl.semaphore_wait(barrier, 7)

    def exchange(buffer, send_sem, recv_sem):
        def copy(source, slot, target):
            return pltpu.make_async_remote_copy(
                src_ref=buffer.at[source],
                dst_ref=buffer.at[source],
                send_sem=send_sem.at[slot],
                recv_sem=recv_sem.at[source],
                device_id=(target, res),
                device_id_type=MESH,
            )

        for slot, peer in enumerate(peers):
            copy(seq, slot, peer).start()
        return copy

    means[seq, 0:16, :] = jnp.sum(kept * normed.astype(F32).reshape(whole), axis=0)
    means[seq, 16:32, :] = jnp.sum(kept, axis=0)
    mean_copy = exchange(means, mean_send, mean_recv)

    weights = weights_ref[...]
    gate = jax.nn.sigmoid(dot(normed, twice(weights, 64)))
    width = weights.shape[1]
    pick_shape = (width, LANES)
    column, at = rows_of(pick_shape), lanes_of(pick_shape)
    tall = dot(flag(row[:, :64] % 64 == lane[:, :64]), weights).astype(BF16)
    same = row // 64 == lane // 64
    key_weights = jnp.where(same, dot(tall, flag(column == 128 + at % 8)), 0.0).astype(BF16)
    value_weights = jnp.where(same, dot(tall, flag(column == 136 + at % 8)), 0.0).astype(BF16)
    query_weights = twice(weights, 0)
    key = dot(normed, key_weights).reshape(whole)
    value = dot(normed, value_weights).reshape(whole)
    head_sum = flag(row // 8 == lane // 8)

    for slot, peer in enumerate(peers):
        mean_copy(peer, slot, seq).wait_recv()
    total = jnp.sum(means[...], axis=0)
    mean = total[:16] / jnp.maximum(total[16:], 1.0)
    mean_query = dot_split(mean, query_weights) * 8**-0.5
    logits = dot_split((key * mean_query[None]).reshape(flat), head_sum).reshape(whole)
    logits = logits + 1000000000.0 * (kept - 1.0)
    peak = jnp.max(logits, axis=0)
    exped = jnp.exp(logits - peak[None])
    sums[seq, 0:16, :] = peak
    sums[seq, 16:32, :] = jnp.sum(exped, axis=0)
    sums[seq, 32:48, :] = jnp.sum(exped * value, axis=0)
    sum_copy = exchange(sums, sum_send, sum_recv)
    for slot, peer in enumerate(peers):
        sum_copy(peer, slot, seq).wait_recv()
    peaks = sums[:, 0:16, :]
    factor = jnp.exp(peaks - jnp.max(peaks, axis=0)[None])
    attended = jnp.sum(factor * sums[:, 32:48, :], axis=0) / jnp.sum(
        factor * sums[:, 16:32, :], axis=0
    )
    gated = (gate.reshape(whole) * attended[None]).astype(BF16).reshape(flat)
    final = line.astype(F32) + dot(gated, twice(exit_col_ref[...], 0))
    results[...] = final.reshape(whole)
    for tile in range(PAIRS):
        out_ref[:, tile * LANES : (tile + 1) * LANES] = results[:, tile, :].astype(BF16)
    for slot in range(7):
        mean_copy(seq, slot, seq).wait_send()
        sum_copy(seq, slot, seq).wait_send()


def on_device(
    extra_activations,
    twofold_representation,
    present_indicator,
    amino_presence,
    twofold_offset_matrix,
    horizontal_matrix,
    horizontal_exit_matrix,
    vertical_matrix,
    vertical_exit_matrix,
):
    vmem = pl.BlockSpec(memory_space=pltpu.VMEM)
    amino_row = amino_presence.reshape(1, RES)
    blocks, biases = pl.pallas_call(
        gather_kernel,
        out_shape=(
            jax.ShapeDtypeStruct((RES, ROWS, LANES), BF16),
            jax.ShapeDtypeStruct((8, 256, LANES), BF16),
        ),
        in_specs=[vmem] * 5,
        out_specs=(vmem, vmem),
        scratch_shapes=[
            pltpu.VMEM((SEQS, PAIRS, LANES), F32),
            pltpu.VMEM((256, LANES), F32),
            pltpu.SemaphoreType.DMA((GROUPS, 31)),
            pltpu.SemaphoreType.DMA((RES, GROUPS)),
            pltpu.SemaphoreType.DMA((7,)),
            pltpu.SemaphoreType.DMA((8,)),
        ],
        compiler_params=pltpu.CompilerParams(
            collective_id=0, has_side_effects=True, vmem_limit_bytes=32 << 20
        ),
        name="gather",
    )(
        extra_activations,
        twofold_representation,
        present_indicator,
        amino_row,
        twofold_offset_matrix,
    )
    gated = pl.pallas_call(
        attend_kernel,
        out_shape=jax.ShapeDtypeStruct((SEQS, 32, LANES), BF16),
        in_specs=[vmem] * 3,
        out_specs=vmem,
        scratch_shapes=[
            pltpu.VMEM((512, 512), F32),
            pltpu.VMEM((SEQS, 512, LANES), BF16),
            pltpu.VMEM((SEQS, 32, LANES), F32),
        ],
        compiler_params=pltpu.CompilerParams(vmem_limit_bytes=40 << 20),
        name="attend",
    )(blocks, biases, horizontal_matrix)
    return pl.pallas_call(
        column_kernel,
        out_shape=jax.ShapeDtypeStruct((SEQS, RES * 64), BF16),
        in_specs=[vmem] * 7,
        out_specs=vmem,
        scratch_shapes=[
            pltpu.VMEM((SEQS, PAIRS, LANES), F32),
            pltpu.VMEM((SEQS, PAIRS, LANES), F32),
            pltpu.VMEM((8, 32, LANES), F32),
            pltpu.VMEM((8, 48, LANES), F32),
            pltpu.SemaphoreType.DMA((7,)),
            pltpu.SemaphoreType.DMA((8,)),
            pltpu.SemaphoreType.DMA((7,)),
            pltpu.SemaphoreType.DMA((8,)),
        ],
        compiler_params=pltpu.CompilerParams(
            collective_id=1, has_side_effects=True, vmem_limit_bytes=32 << 20
        ),
        name="column",
    )(
        extra_activations,
        gated,
        present_indicator,
        amino_row,
        horizontal_exit_matrix,
        vertical_matrix,
        vertical_exit_matrix,
    )


def solution(mesh):
    in_specs = (
        P("seq", "res"),
        P("res", "seq", None),
        P("seq", "res"),
        P("res"),
        P(),
        P(),
        P(),
        P(),
        P(),
    )
    out_specs = P("seq", "res")
    return jax.shard_map(
        on_device, mesh=mesh, in_specs=in_specs, out_specs=out_specs, check_vma=False
    )
```

```python
import jax
import jax.numpy as jnp
from jax import lax
from jax.experimental import pallas as pl
from jax.experimental.pallas import tpu as pltpu
from jax.sharding import PartitionSpec as P

MESH = pl.DeviceIdType.MESH
F32, BF16 = jnp.float32, jnp.bfloat16
SEQS, RES, PAIRS, LANES = 32, 32, 16, 128
ROWS = PAIRS + SEQS * PAIRS
GROUPS = 4
PER_GROUP = SEQS // GROUPS
LOG2E = 1.4426950408889634
SPANS = [
    (0 if g == 0 else PAIRS + g * PER_GROUP * PAIRS, PER_GROUP * PAIRS + (PAIRS if g == 0 else 0)) for g in range(GROUPS)
]


def rows_of(shape):
    return lax.broadcasted_iota(jnp.int32, shape, 0)


def lanes_of(shape):
    return lax.broadcasted_iota(jnp.int32, shape, 1)


def flag(condition):
    return jnp.where(condition, 1.0, 0.0).astype(BF16)


def dot(left, right):
    return jnp.dot(left, right, preferred_element_type=F32)


def dot_nt(left, right):
    return lax.dot_general(left, right, (((1,), (1,)), ((), ())), preferred_element_type=F32)


def dot_split(left, right):
    high = left.astype(BF16)
    low = (left - high.astype(F32)).astype(BF16)
    return dot(high, right) + dot(low, right)


def normalize(values, width, coarse=False):
    shape = (LANES, LANES)
    average = jnp.where(
        rows_of(shape) // width == lanes_of(shape) // width, 1.0 / width, 0.0
    ).astype(BF16)
    centre = values.astype(F32) - dot(values, average)
    squares = centre * centre
    spread = dot(squares.astype(BF16), average) if coarse else dot_split(squares, average)
    return centre * lax.rsqrt(spread + 1e-05)


def tile_rows(weights, shift):
    height, width = weights.shape
    tall = dot(flag(rows_of((LANES, height)) % height == lanes_of((LANES, height))), weights)
    column = rows_of((width, LANES))
    pick = flag(column == lanes_of((width, LANES)) % 64 + shift)
    return dot(tall.astype(BF16), pick)


def twice(weights, shift):
    shape = (LANES, LANES)
    return jnp.where(
        rows_of(shape) // 64 == lanes_of(shape) // 64, tile_rows(weights, shift), 0.0
    ).astype(BF16)


SCHEDULE = [
    (1, "far", 1),
    (1, "next", 2),
    (3, "core", 1),
    (4, "far", 2),
    (4, "next", 3),
    (7, "core", 2),
    (7, "far", 3),
    (11, "core", 3),
]


def fused_kernel(
    x_hbm,
    pair_hbm,
    present_hbm,
    amino_hbm,
    offset_hbm,
    weights_hbm,
    exit_hbm,
    column_hbm,
    exit_col_hbm,
    out_ref,
    x_ref,
    pair_ref,
    present_ref,
    amino_ref,
    offset_ref,
    weights_ref,
    exit_ref,
    column_ref,
    exit_col_ref,
    blocks,
    biases,
    lines,
    offsets,
    bias,
    queries,
    gates,
    gateds,
    logits_even,
    logits_odd,
    peak_even,
    peak_odd,
    kepts,
    results,
    means,
    sums,
    load_sem,
    send_sem,
    z_recv,
    y_recv,
    far_recv,
    core_recv,
    bias_send,
    bias_recv,
    mean_send,
    mean_recv,
    sum_send,
    sum_recv,
):
    loads = [
        pltpu.make_async_copy(source, target, load_sem.at[slot])
        for slot, (source, target) in enumerate(
            [
                (pair_hbm, pair_ref),
                (offset_hbm, offset_ref),
                (x_hbm, x_ref),
                (present_hbm, present_ref),
                (amino_hbm, amino_ref),
                (weights_hbm, weights_ref),
                (exit_hbm, exit_ref),
                (column_hbm, column_ref),
                (exit_col_hbm, exit_col_ref),
            ]
        )
    ]
    for load in loads:
        load.start()
    seq, res = lax.axis_index("seq"), lax.axis_index("res")
    core, y, z = res % 2, (res // 2) % 4, res // 8
    up, down, across = (y + 1) % 4, (y + 3) % 4, (y + 2) % 4
    partner = seq // 2 * 2 + (1 - seq % 2)
    bias_peers = [partner] + [(seq + 2 * d) % 8 for d in (1, 2, 3)]
    seq_peers = [(seq + d) % 8 for d in range(1, 8)]

    def place(z_at, y_at, core_at):
        return (z_at * 4 + y_at) * 2 + core_at

    z_peers = [place((z + d) % 4, y, core) for d in (1, 2, 3)]
    up_peer, down_peer, core_peer = place(z, up, core), place(z, down, core), place(z, y, 1 - core)
    res_peers = z_peers + [up_peer, down_peer, core_peer]
    barrier = pltpu.get_barrier_semaphore()
    for peer in seq_peers:
        pl.semaphore_signal(barrier, inc=1, device_id=(peer, res), device_id_type=MESH)
    for peer in res_peers:
        pl.semaphore_signal(barrier, inc=1, device_id=(seq, peer), device_id_type=MESH)

    loads[0].wait()
    loads[1].wait()

    def bias_rows(step, carry):
        pair = pair_ref[pl.ds(step * 4, 4)].reshape(4 * LANES, LANES)
        normed = normalize(pair, LANES, coarse=True).astype(BF16)
        found = dot_nt(offset_ref[...], normed)
        for row in range(4):
            offsets[pl.ds(pl.multiple_of(step * 32 + row * 8, 8), 8), :] = found[
                :, row * LANES : (row + 1) * LANES
            ]
        return carry

    lax.fori_loop(0, 8, bias_rows, 0, unroll=2)
    for head in range(8):
        for parity in range(2):
            biases[seq, pl.ds(head * 32 + parity * 16, 16), :] = offsets[
                pl.ds(parity * 8 + head, 16, stride=16), :
            ].astype(BF16)

    whole = (SEQS, PAIRS, LANES)
    flat = (SEQS * PAIRS, LANES)
    for load in loads[2:5]:
        load.wait()
    for tile in range(PAIRS):
        lines[:, tile, :] = x_ref[:, tile * LANES : (tile + 1) * LANES].astype(F32)
    own = normalize(lines[...].reshape(flat).astype(BF16), 64).astype(BF16)
    blocks[z, y, core, PAIRS:ROWS, :] = own
    kept = (present_ref[...] * amino_ref[...]).astype(F32).astype(BF16)
    turned = jnp.zeros((PAIRS, LANES), F32)
    for parity in range(2):
        shape = (PAIRS, SEQS)
        picked = dot_nt(flag(lanes_of(shape) == 2 * rows_of(shape) + parity), kept)
        shape = (SEQS, LANES)
        turned += dot(
            picked.astype(BF16), flag(lanes_of(shape) == rows_of(shape) + parity * SEQS)
        )
    blocks[z, y, core, 0:PAIRS, :] = jnp.where(
        lanes_of((PAIRS, LANES)) < 64, 1000000000.0 * (turned - 1.0), 1.0
    ).astype(BF16)

    def remote(view, send, recv, target):
        return pltpu.make_async_remote_copy(
            src_ref=view,
            dst_ref=view,
            send_sem=send,
            recv_sem=recv,
            device_id=(seq, target),
            device_id_type=MESH,
        )

    def one(z_at, group):
        return blocks.at[z_at, y, core, pl.ds(*SPANS[group]), :]

    def column(y_at, core_at, group, first=0, count=4):
        return blocks.at[pl.ds(first, count), y_at, core_at, pl.ds(*SPANS[group]), :]

    def z_copy(group, d):
        return remote(one(z, group), send_sem.at[group, d - 1], z_recv.at[z, group], z_peers[d - 1])

    def z_wait(group, d):
        at = (z + d) % 4
        remote(one(at, group), send_sem.at[group, 0], z_recv.at[at, group], res).wait_recv()

    def y_copy(group, side, source):
        target = (up_peer, down_peer)[side]
        return remote(
            column(source, core, group),
            send_sem.at[group, 3 + side],
            y_recv.at[1 - side, group],
            target,
        )

    def far_copy(group, side, source):
        target = (up_peer, down_peer)[side]
        return remote(
            column(source, core, group, 2 * side, 2),
            send_sem.at[group, 5 + side],
            far_recv.at[side, group],
            target,
        )

    def core_copy(group, slot, source, core_at):
        return remote(
            column(source, core_at, group),
            send_sem.at[group, 7 + slot],
            core_recv.at[source, group],
            core_peer,
        )

    def stage_near(group):
        for d in (1, 2, 3):
            z_wait(group, d)
        y_copy(group, 0, y).start()
        y_copy(group, 1, y).start()
        core_copy(group, 0, y, core).start()

    def stage_next(group):
        y_copy(group, 0, down).wait_recv()
        far_copy(group, 0, down).start()
        core_copy(group, 1, down, core).start()
        y_copy(group, 1, up).wait_recv()
        far_copy(group, 1, up).start()
        core_copy(group, 2, up, core).start()

    def stage_far(group):
        far_copy(group, 0, across).wait_recv()
        far_copy(group, 1, across).wait_recv()
        core_copy(group, 3, across, core).start()

    def stage_core(group):
        for at in range(4):
            core_copy(group, 0, at, 1 - core).wait_recv()

    def bias_copy(block, slot, target):
        return pltpu.make_async_remote_copy(
            src_ref=biases.at[block],
            dst_ref=biases.at[block],
            send_sem=bias_send.at[slot],
            recv_sem=bias_recv.at[block],
            device_id=(target, res),
            device_id_type=MESH,
        )

    pl.semaphore_wait(barrier, len(seq_peers) + len(res_peers))
    for d in (1, 2, 3):
        z_copy(0, d).start()
    for slot, peer in enumerate(bias_peers):
        bias_copy(seq, slot, peer).start()
    for group in range(1, GROUPS):
        for d in (1, 2, 3):
            z_copy(group, d).start()

    for load in loads[5:]:
        load.wait()
    weights = weights_ref[...]
    square = (LANES, LANES)
    row, lane = rows_of(square), lanes_of(square)
    wide = (LANES, 256)
    turned = dot_nt(flag(lanes_of(wide) == rows_of(wide) % 64 + 64), weights).astype(BF16)
    shape = (64, LANES)
    turned = dot(turned, flag(rows_of(shape) == lanes_of(shape) % 64))
    query_weights = tile_rows(weights, 0)
    gate_weights = tile_rows(weights, 192)

    def query_side(side):
        mine = row // 64 == side
        query = dot(own, jnp.where(mine, query_weights, 0.0).astype(BF16))
        query = (query * (LOG2E * 8**-0.5)).astype(BF16)
        gate = dot(own, jnp.where(mine, gate_weights, 0.0).astype(BF16))
        gates[:, side * 16 : side * 16 + 16, :] = jax.nn.sigmoid(gate).reshape(whole)
        for head in range(8):
            keyed = jnp.where(row // 8 == head, turned, 0.0)
            both = jnp.concatenate(
                [jnp.where(lane // 64 == parity, keyed, 0.0) for parity in range(2)], axis=1
            ).astype(BF16)
            found = dot(query, both).astype(BF16)
            for parity in range(2):
                start = (parity * 8 + head) * 32 + side * 16
                queries[:, start : start + 16, :] = found[
                    :, parity * LANES : (parity + 1) * LANES
                ].reshape(whole)

    query_side(0)
    stage_near(0)
    query_side(1)
    stage_near(1)
    bias_copy(partner, 0, seq).wait_recv()
    for slot, peer in enumerate(bias_peers[1:]):
        bias_copy(partner, 4 + slot, peer).start()

    spread = (RES, RES * 64)
    kept = dot(kept, flag(rows_of(spread) == lanes_of(spread) // 64))
    for tile in range(PAIRS):
        kepts[:, tile, :] = kept[:, tile * LANES : (tile + 1) * LANES]

    stage_next(0)
    stage_near(2)
    stage_far(0)
    stage_near(3)
    stage_next(1)
    for peer in bias_peers[1:]:
        bias_copy(peer, 0, seq).wait_recv()
        bias_copy(peer // 2 * 2 + (1 - peer % 2), 0, seq).wait_recv()
    shape = (256, 256)
    order = flag(rows_of(shape) == 2 * (lanes_of(shape) % LANES) + lanes_of(shape) // LANES)
    for tile in range(4):
        both = jnp.concatenate([biases[2 * tile], biases[2 * tile + 1]], axis=1)
        placed = dot(both, order) * LOG2E
        for parity in range(2):
            bias[parity * 256 : parity * 256 + 256, tile * LANES : (tile + 1) * LANES] = placed[
                :, parity * LANES : (parity + 1) * LANES
            ]
    stage_core(0)

    value_weights = jnp.where(lane >= 64, tile_rows(weights, 128), 0.0).astype(BF16)
    half = lanes_of((256, LANES)) < 64
    head_of = lanes_of((32, LANES)) // 8 - 8

    def keys_of(line):
        start = pl.multiple_of(PAIRS + line * PAIRS, PAIRS)
        keys = blocks[:, :, :, pl.ds(start, PAIRS), :].reshape(512, LANES)
        mask = blocks[:, :, :, 0:PAIRS, :].reshape(512, LANES)
        return jnp.concatenate([keys, mask], axis=1)

    def score(line, logits_ref, peak_ref):
        at = lanes_of((PAIRS, LANES))
        picks = [flag(at == line)] * 16 + [flag(at == line + SEQS)] * 16
        left = jnp.concatenate([queries[line], jnp.concatenate(picks, axis=0)], axis=1)
        logits = dot_nt(left, keys_of(line)) + bias[...]
        logits_ref[...] = logits
        peak = jnp.maximum(
            jnp.maximum(logits[:, 0:128], logits[:, 128:256]),
            jnp.maximum(logits[:, 256:384], logits[:, 384:512]),
        )
        peak = jnp.max(jnp.maximum(peak[:256], peak[256:]), axis=1, keepdims=True)
        peak_ref[...] = jnp.broadcast_to(peak, (256, LANES))

    def weigh(line, logits_ref, peak_ref):
        peak = jnp.concatenate([peak_ref[...]] * 4, axis=1)
        peak = jnp.concatenate([peak, peak], axis=0)
        exped = jnp.exp2(logits_ref[...] - peak).astype(BF16)
        summed = dot(exped, keys_of(line))
        taken = jnp.where(half, summed[:256, :LANES], summed[256:, :LANES]).astype(BF16)
        total = summed[:256, LANES:] + summed[256:, LANES:]
        found = dot(taken, value_weights) / total
        attended = jnp.zeros((32, LANES), F32)
        for head in range(8):
            attended = jnp.where(head_of == head, found[head * 32 : head * 32 + 32], attended)
        gateds[line] = (gates[line] * attended).astype(BF16)

    score(0, logits_even, peak_even)

    def two_lines(step, carry):
        for at, stage, group in SCHEDULE:

            @pl.when(step == at)
            def _():
                {"next": stage_next, "far": stage_far, "core": stage_core}[stage](group)

        line = 2 * step
        score(line + 1, logits_odd, peak_odd)
        weigh(line, logits_even, peak_even)
        score(jnp.minimum(line + 2, SEQS - 1), logits_even, peak_even)
        weigh(line + 1, logits_odd, peak_odd)
        return carry

    lax.fori_loop(0, SEQS // 2, two_lines, 0)

    exits = tile_rows(exit_ref[...], 0)
    update = jnp.zeros(flat, F32)
    for side in range(2):
        exit_side = jnp.where((row >= 64) & (lane // 64 == side), exits, 0.0).astype(BF16)
        update += dot(gateds[:, side * 16 : side * 16 + 16, :].reshape(flat), exit_side)
    line = (lines[...].reshape(flat) + update).astype(BF16)
    normed = normalize(line, 64).astype(BF16)

    def exchange(buffer, send, recv):
        def copy(source, slot, target):
            return pltpu.make_async_remote_copy(
                src_ref=buffer.at[source],
                dst_ref=buffer.at[source],
                send_sem=send.at[slot],
                recv_sem=recv.at[source],
                device_id=(target, res),
                device_id_type=MESH,
            )

        for slot, peer in enumerate(seq_peers):
            copy(seq, slot, peer).start()
        return copy

    kept = kepts[...]
    means[seq, 0:16, :] = jnp.sum(kept * normed.astype(F32).reshape(whole), axis=0)
    means[seq, 16:32, :] = jnp.sum(kept, axis=0)
    mean_copy = exchange(means, mean_send, mean_recv)

    weights = column_ref[...]
    gate = jax.nn.sigmoid(dot(normed, twice(weights, 64)))
    pick_shape = (weights.shape[1], LANES)
    source, at = rows_of(pick_shape), lanes_of(pick_shape)
    tall = dot(flag(row[:, :64] % 64 == lane[:, :64]), weights).astype(BF16)
    same = row // 64 == lane // 64
    key_weights = jnp.where(same, dot(tall, flag(source == 128 + at % 8)), 0.0).astype(BF16)
    value_weights = jnp.where(same, dot(tall, flag(source == 136 + at % 8)), 0.0).astype(BF16)
    query_weights = twice(weights, 0)
    key = dot(normed, key_weights).reshape(whole)
    value = dot(normed, value_weights).reshape(whole)
    head_sum = flag(row // 8 == lane // 8)

    for slot, peer in enumerate(seq_peers):
        mean_copy(peer, slot, seq).wait_recv()
    total = jnp.sum(means[...], axis=0)
    mean = total[:16] / jnp.maximum(total[16:], 1.0)
    mean_query = dot_split(mean, query_weights) * 8**-0.5
    logits = dot_split((key * mean_query[None]).reshape(flat), head_sum).reshape(whole)
    logits = logits + 1000000000.0 * (kept - 1.0)
    peak = jnp.max(logits, axis=0)
    exped = jnp.exp(logits - peak[None])
    sums[seq, 0:16, :] = peak
    sums[seq, 16:32, :] = jnp.sum(exped, axis=0)
    sums[seq, 32:48, :] = jnp.sum(exped * value, axis=0)
    sum_copy = exchange(sums, sum_send, sum_recv)
    for slot, peer in enumerate(seq_peers):
        sum_copy(peer, slot, seq).wait_recv()
    peaks = sums[:, 0:16, :]
    factor = jnp.exp(peaks - jnp.max(peaks, axis=0)[None])
    attended = jnp.sum(factor * sums[:, 32:48, :], axis=0) / jnp.sum(
        factor * sums[:, 16:32, :], axis=0
    )
    gated = (gate.reshape(whole) * attended[None]).astype(BF16).reshape(flat)
    final = line.astype(F32) + dot(gated, twice(exit_col_ref[...], 0))
    results[...] = final.reshape(whole)
    for tile in range(PAIRS):
        out_ref[:, tile * LANES : (tile + 1) * LANES] = results[:, tile, :].astype(BF16)

    for slot in range(7):
        bias_copy(seq, slot, seq).wait_send()
        mean_copy(seq, slot, seq).wait_send()
        sum_copy(seq, slot, seq).wait_send()
    for group in range(GROUPS):
        for d in (1, 2, 3):
            z_copy(group, d).wait_send()
        for side in range(2):
            y_copy(group, side, y).wait_send()
            far_copy(group, side, y).wait_send()
        for slot in range(4):
            core_copy(group, slot, y, core).wait_send()


def on_device(
    extra_activations,
    twofold_representation,
    present_indicator,
    amino_presence,
    twofold_offset_matrix,
    horizontal_matrix,
    horizontal_exit_matrix,
    vertical_matrix,
    vertical_exit_matrix,
):
    operands = [
        extra_activations,
        twofold_representation,
        present_indicator,
        amino_presence.reshape(1, RES),
        twofold_offset_matrix.T,
        horizontal_matrix,
        horizontal_exit_matrix,
        vertical_matrix,
        vertical_exit_matrix,
    ]
    dma, vmem = pltpu.SemaphoreType.DMA, pltpu.VMEM
    return pl.pallas_call(
        fused_kernel,
        out_shape=jax.ShapeDtypeStruct((SEQS, RES * 64), BF16),
        in_specs=[pl.BlockSpec(memory_space=pltpu.HBM)] * len(operands),
        out_specs=pl.BlockSpec(memory_space=vmem),
        scratch_shapes=[vmem(operand.shape, operand.dtype) for operand in operands]
        + [
            vmem((4, 4, 2, ROWS, LANES), BF16),
            vmem((8, 256, LANES), BF16),
            vmem((SEQS, PAIRS, LANES), F32),
            vmem((256, LANES), F32),
            vmem((512, 512), F32),
            vmem((SEQS, 512, LANES), BF16),
            vmem((SEQS, 32, LANES), F32),
            vmem((SEQS, 32, LANES), BF16),
            vmem((512, 512), F32),
            vmem((512, 512), F32),
            vmem((256, LANES), F32),
            vmem((256, LANES), F32),
            vmem((SEQS, PAIRS, LANES), F32),
            vmem((SEQS, PAIRS, LANES), F32),
            vmem((8, 32, LANES), F32),
            vmem((8, 48, LANES), F32),
            dma((len(operands),)),
            dma((GROUPS, 11)),
            dma((4, GROUPS)),
            dma((2, GROUPS)),
            dma((2, GROUPS)),
            dma((4, GROUPS)),
            dma((7,)),
            dma((8,)),
            dma((7,)),
            dma((8,)),
            dma((7,)),
            dma((8,)),
        ],
        compiler_params=pltpu.CompilerParams(
            collective_id=0, has_side_effects=True, vmem_limit_bytes=48 << 20
        ),
        name="fused",
    )(*operands)


def solution(mesh):
    in_specs = (
        P("seq", "res"),
        P("res", "seq", None),
        P("seq", "res"),
        P("res"),
        P(),
        P(),
        P(),
        P(),
        P(),
    )
    out_specs = P("seq", "res")
    return jax.shard_map(
        on_device, mesh=mesh, in_specs=in_specs, out_specs=out_specs, check_vma=False
    )
```

```python
import jax
import jax.numpy as jnp
from jax import lax
from jax.experimental import pallas as pl
from jax.experimental.pallas import tpu as pltpu
from jax.sharding import PartitionSpec as P

MESH = pl.DeviceIdType.MESH
F32, BF16 = jnp.float32, jnp.bfloat16
SEQS, RES, PAIRS, LANES = 32, 32, 16, 128
ROWS = PAIRS + SEQS * PAIRS
COUNTS = (4, 8, 10, 10)
GROUPS = len(COUNTS)
LOG2E = 1.4426950408889634
SPANS = [
    (0 if g == 0 else PAIRS * (1 + sum(COUNTS[:g])), PAIRS * (COUNTS[g] + (g == 0)))
    for g in range(GROUPS)
]


def rows_of(shape):
    return lax.broadcasted_iota(jnp.int32, shape, 0)


def lanes_of(shape):
    return lax.broadcasted_iota(jnp.int32, shape, 1)


def flag(condition):
    return jnp.where(condition, 1.0, 0.0).astype(BF16)


def dot(left, right):
    return jnp.dot(left, right, preferred_element_type=F32)


def dot_nt(left, right):
    return lax.dot_general(left, right, (((1,), (1,)), ((), ())), preferred_element_type=F32)


def dot_split(left, right):
    high = left.astype(BF16)
    low = (left - high.astype(F32)).astype(BF16)
    return dot(high, right) + dot(low, right)


def normalize(values, width):
    shape = (LANES, LANES)
    average = jnp.where(
        rows_of(shape) // width == lanes_of(shape) // width, 1.0 / width, 0.0
    ).astype(BF16)
    centre = values.astype(F32) - dot(values, average)
    squares = centre * centre
    spread = dot_split(squares, average)
    return centre * lax.rsqrt(spread + 1e-05)


def tile_rows(weights, shift):
    height, width = weights.shape
    tall = dot(flag(rows_of((LANES, height)) % height == lanes_of((LANES, height))), weights)
    column = rows_of((width, LANES))
    pick = flag(column == lanes_of((width, LANES)) % 64 + shift)
    return dot(tall.astype(BF16), pick)


def twice(weights, shift):
    shape = (LANES, LANES)
    return jnp.where(
        rows_of(shape) // 64 == lanes_of(shape) // 64, tile_rows(weights, shift), 0.0
    ).astype(BF16)


SCHEDULE = [
    (1, "core", 1),
    (3, "next", 2),
    (3, "near", 3),
    (5, "core", 2),
    (7, "next", 3),
    (10, "core", 3),
]


def fused_kernel(
    x_hbm,
    pair_hbm,
    present_hbm,
    amino_hbm,
    offset_hbm,
    weights_hbm,
    exit_hbm,
    column_hbm,
    exit_col_hbm,
    out_ref,
    x_ref,
    pair_ref,
    present_ref,
    amino_ref,
    offset_ref,
    weights_ref,
    exit_ref,
    column_ref,
    exit_col_ref,
    blocks,
    biases,
    lines,
    offsets,
    bias,
    queries,
    gates,
    gateds,
    logits_even,
    logits_odd,
    peak_even,
    peak_odd,
    taken_even,
    taken_odd,
    total_even,
    total_odd,
    kepts,
    results,
    means,
    sums,
    load_sem,
    send_sem,
    own_send,
    own_recv,
    z_recv,
    y_recv,
    core_recv,
    bias_send,
    bias_recv,
    mean_send,
    mean_recv,
    sum_send,
    sum_recv,
):
    loads = [
        pltpu.make_async_copy(source, target, load_sem.at[slot])
        for slot, (source, target) in enumerate(
            [
                (x_hbm, x_ref),
                (present_hbm, present_ref),
                (amino_hbm, amino_ref),
                (pair_hbm, pair_ref),
                (offset_hbm, offset_ref),
                (weights_hbm, weights_ref),
                (exit_hbm, exit_ref),
                (column_hbm, column_ref),
                (exit_col_hbm, exit_col_ref),
            ]
        )
    ]
    for load in loads:
        load.start()
    seq, res = lax.axis_index("seq"), lax.axis_index("res")
    core, y, z = res % 2, (res // 2) % 4, res // 8
    up, down, across = (y + 1) % 4, (y + 3) % 4, (y + 2) % 4
    partner = seq // 2 * 2 + (1 - seq % 2)
    bias_peers = [partner] + [(seq + 2 * d) % 8 for d in (1, 2, 3)]
    seq_peers = [(seq + d) % 8 for d in range(1, 8)]

    def place(z_at, y_at, core_at):
        return (z_at * 4 + y_at) * 2 + core_at

    z_peers = [place((z + d) % 4, y, core) for d in (1, 2, 3)]
    up_peer, down_peer, core_peer = place(z, up, core), place(z, down, core), place(z, y, 1 - core)
    across_peer = place(z, across, core)
    res_peers = z_peers + [up_peer, down_peer, across_peer, core_peer]
    barrier = pltpu.get_barrier_semaphore()
    for peer in seq_peers:
        pl.semaphore_signal(barrier, inc=1, device_id=(peer, res), device_id_type=MESH)
    for peer in res_peers:
        pl.semaphore_signal(barrier, inc=1, device_id=(seq, peer), device_id_type=MESH)

    whole = (SEQS, PAIRS, LANES)
    flat = (SEQS * PAIRS, LANES)
    for load in loads[0:3]:
        load.wait()
    for tile in range(PAIRS):
        lines[:, tile, :] = x_ref[:, tile * LANES : (tile + 1) * LANES].astype(F32)
    own = normalize(lines[...].reshape(flat).astype(BF16), 64).astype(BF16)
    blocks[0, y, core, PAIRS:ROWS, :] = own
    kept = (present_ref[...] * amino_ref[...]).astype(F32).astype(BF16)
    turned = jnp.zeros((PAIRS, LANES), F32)
    counted = jnp.zeros((PAIRS, LANES), F32)
    for parity in range(2):
        shape = (PAIRS, SEQS)
        picked = dot_nt(flag(lanes_of(shape) == 2 * rows_of(shape) + parity), kept)
        shape = (SEQS, LANES)
        turned += dot(
            picked.astype(BF16), flag(lanes_of(shape) == rows_of(shape) + parity * SEQS)
        )
        counted += dot(picked.astype(BF16), flag(lanes_of(shape) // 64 == parity))
    biases[seq, 256:272, :] = counted.astype(BF16)
    blocks[0, y, core, 0:PAIRS, :] = jnp.where(
        lanes_of((PAIRS, LANES)) < 64, 1000000000.0 * (turned - 1.0), 1.0
    ).astype(BF16)

    def remote(view, send, recv, target):
        return pltpu.make_async_remote_copy(
            src_ref=view,
            dst_ref=view,
            send_sem=send,
            recv_sem=recv,
            device_id=(seq, target),
            device_id_type=MESH,
        )

    def column(y_at, core_at, group, first=0, count=4):
        return blocks.at[pl.ds(first, count), y_at, core_at, pl.ds(*SPANS[group]), :]

    def z_copy(group, d):
        rows = pl.ds(*SPANS[group])
        return pltpu.make_async_remote_copy(
            src_ref=blocks.at[0, y, core, rows, :],
            dst_ref=blocks.at[4 - d, y, core, rows, :],
            send_sem=send_sem.at[group, d - 1],
            recv_sem=z_recv.at[4 - d, group],
            device_id=(seq, z_peers[d - 1]),
            device_id_type=MESH,
        )

    def own_copy(side, source):
        target = (up_peer, down_peer, across_peer, core_peer)[side]
        return remote(
            blocks.at[0, source, core] if side < 3 else blocks.at[0, y, source],
            own_send.at[side],
            own_recv.at[(1, 0, 2, 3)[side]],
            target,
        )

    def y_copy(group, side, source):
        target = (up_peer, down_peer, across_peer)[side]
        return remote(
            column(source, core, group, 1, 3),
            send_sem.at[group, 3 + side],
            y_recv.at[(1, 0, 2)[side], group],
            target,
        )

    def core_copy(group, slot, source, core_at):
        first = 1 if slot == 0 else 0
        return remote(
            column(source, core_at, group, first, 4 - first),
            send_sem.at[group, 6 + slot],
            core_recv.at[slot, group],
            core_peer,
        )

    def stage_near(group):
        for d in (1, 2, 3):
            z_copy(group, d).wait_recv()
        if group + 1 < GROUPS:
            for d in (1, 2, 3):
                z_copy(group + 1, d).start()
        for side in range(3):
            y_copy(group, side, y).start()
        core_copy(group, 0, y, core).start()

    def stage_next(group):
        for side, source in enumerate((down, up, across)):
            if group == 0:
                own_copy(side, source).wait_recv()
            y_copy(group, side, source).wait_recv()
            core_copy(group, side + 1, source, core).start()

    def stage_core(group):
        if group == 0:
            own_copy(3, 1 - core).wait_recv()
        for slot, at in enumerate((y, down, up, across)):
            core_copy(group, slot, at, 1 - core).wait_recv()

    def bias_copy(block, slot, target):
        return pltpu.make_async_remote_copy(
            src_ref=biases.at[block],
            dst_ref=biases.at[block],
            send_sem=bias_send.at[slot],
            recv_sem=bias_recv.at[block],
            device_id=(target, res),
            device_id_type=MESH,
        )

    pl.semaphore_wait(barrier, len(seq_peers) + len(res_peers))
    for side in range(3):
        own_copy(side, y).start()
    for d in (1, 2, 3):
        z_copy(0, d).start()
    own_copy(3, core).start()

    for load in loads[3:5]:
        load.wait()

    shape = (256, 256)
    average = jnp.where(
        rows_of(shape) // LANES == lanes_of(shape) // LANES, 1.0 / LANES, 0.0
    ).astype(BF16)

    def bias_rows(step, carry):
        pair = pair_ref[pl.ds(step * 4, 4)].reshape(4 * LANES, LANES)
        pair = jnp.concatenate([pair[:256], pair[256:]], axis=1)
        centre = pair.astype(F32) - dot(pair, average)
        spread = dot((centre * centre).astype(BF16), average)
        normed = (centre * lax.rsqrt(spread + 1e-05)).astype(BF16)
        for row in range(4):
            start = row // 2 * LANES
            found = dot_nt(
                offset_ref[...],
                normed[row % 2 * LANES : row % 2 * LANES + LANES, start : start + LANES],
            )
            offsets[pl.ds(pl.multiple_of(step * 32 + row * 8, 8), 8), :] = found
        return carry

    lax.fori_loop(0, 8, bias_rows, 0, unroll=2)
    for head in range(8):
        for parity in range(2):
            biases[seq, pl.ds(head * 32 + parity * 16, 16), :] = offsets[
                pl.ds(parity * 8 + head, 16, stride=16), :
            ].astype(BF16)

    for slot, peer in enumerate(bias_peers):
        bias_copy(seq, slot, peer).start()

    for load in loads[5:]:
        load.wait()
    weights = weights_ref[...]
    square = (LANES, LANES)
    row, lane = rows_of(square), lanes_of(square)
    wide = (LANES, 256)
    turned = dot_nt(flag(lanes_of(wide) == rows_of(wide) % 64 + 64), weights).astype(BF16)
    shape = (64, LANES)
    turned = dot(turned, flag(rows_of(shape) == lanes_of(shape) % 64))
    query_weights = tile_rows(weights, 0)
    gate_weights = tile_rows(weights, 192)

    def query_side(side):
        mine = row // 64 == side
        query = dot(own, jnp.where(mine, query_weights, 0.0).astype(BF16))
        query = (query * (LOG2E * 8**-0.5)).astype(BF16)
        gate = dot(own, jnp.where(mine, gate_weights, 0.0).astype(BF16))
        gates[:, side * 16 : side * 16 + 16, :] = jax.nn.sigmoid(gate).reshape(whole)
        for head in range(8):
            keyed = jnp.where(row // 8 == head, turned, 0.0)
            both = jnp.concatenate(
                [jnp.where(lane // 64 == parity, keyed, 0.0) for parity in range(2)], axis=1
            ).astype(BF16)
            found = dot(query, both).astype(BF16)
            for parity in range(2):
                start = (parity * 8 + head) * 32 + side * 16
                queries[:, start : start + 16, :] = found[
                    :, parity * LANES : (parity + 1) * LANES
                ].reshape(whole)

    stage_near(0)
    query_side(0)
    query_side(1)
    stage_next(0)
    bias_copy(partner, 0, seq).wait_recv()
    for slot, peer in enumerate(bias_peers[1:]):
        bias_copy(partner, 4 + slot, peer).start()
    stage_near(1)

    spread = (RES, RES * 64)
    kept = dot(kept, flag(rows_of(spread) == lanes_of(spread) // 64))
    for tile in range(PAIRS):
        kepts[:, tile, :] = kept[:, tile * LANES : (tile + 1) * LANES]

    for peer in bias_peers[1:]:
        bias_copy(peer, 0, seq).wait_recv()
        bias_copy(peer // 2 * 2 + (1 - peer % 2), 0, seq).wait_recv()
    shape = (256, 256)
    order = flag(rows_of(shape) == 2 * (lanes_of(shape) % LANES) + lanes_of(shape) // LANES)
    for tile in range(4):
        at = (z + tile) % 4
        both = jnp.concatenate([biases[2 * at, 0:256], biases[2 * at + 1, 0:256]], axis=1)
        placed = dot(both, order) * LOG2E
        for parity in range(2):
            bias[parity * 256 : parity * 256 + 256, tile * LANES : (tile + 1) * LANES] = placed[
                :, parity * LANES : (parity + 1) * LANES
            ]
    stage_core(0)
    stage_next(1)
    stage_near(2)

    value_weights = jnp.where(lane >= 64, tile_rows(weights, 128), 0.0).astype(BF16)
    half = lanes_of((256, LANES)) < 64
    head_of = lanes_of((32, LANES)) // 8 - 8

    def keys_of(line):
        start = pl.multiple_of(PAIRS + line * PAIRS, PAIRS)
        keys = blocks[:, :, :, pl.ds(start, PAIRS), :].reshape(512, LANES)
        mask = blocks[:, :, :, 0:PAIRS, :].reshape(512, LANES)
        return jnp.concatenate([keys, mask], axis=1)

    def score(line, logits_ref, peak_ref):
        at = lanes_of((PAIRS, LANES))
        picks = [flag(at == line)] * 16 + [flag(at == line + SEQS)] * 16
        left = jnp.concatenate([queries[line], jnp.concatenate(picks, axis=0)], axis=1)
        logits = dot_nt(left, keys_of(line)) + bias[...]
        logits_ref[...] = logits
        peak = jnp.maximum(
            jnp.maximum(logits[:, 0:128], logits[:, 128:256]),
            jnp.maximum(logits[:, 256:384], logits[:, 384:512]),
        )
        peak = jnp.max(jnp.maximum(peak[:256], peak[256:]), axis=1, keepdims=True)
        peak_ref[...] = jnp.broadcast_to(peak, (256, LANES))

    def weigh(line, logits_ref, peak_ref, taken_ref, total_ref):
        peak = jnp.concatenate([peak_ref[...]] * 4, axis=1)
        peak = jnp.concatenate([peak, peak], axis=0)
        exped = jnp.exp2(logits_ref[...] - peak).astype(BF16)
        summed = dot(exped, keys_of(line))
        taken_ref[...] = jnp.where(half, summed[:256, :LANES], summed[256:, :LANES]).astype(BF16)
        total_ref[...] = summed[:256, LANES:] + summed[256:, LANES:]

    def finish(line, taken_ref, total_ref):
        found = dot(taken_ref[...], value_weights) / total_ref[...]
        attended = jnp.zeros((32, LANES), F32)
        for head in range(8):
            attended = jnp.where(head_of == head, found[head * 32 : head * 32 + 32], attended)
        gateds[line] = (gates[line] * attended).astype(BF16)

    stages = {"near": stage_near, "next": stage_next, "core": stage_core}
    score(0, logits_even, peak_even)

    def two_lines(step, carry):
        for at, stage, group in SCHEDULE:

            @pl.when(step == at)
            def _():
                stages[stage](group)

        line = 2 * step
        score(line + 1, logits_odd, peak_odd)
        weigh(line, logits_even, peak_even, taken_even, total_even)
        finish(jnp.maximum(line - 1, 0), taken_odd, total_odd)
        score(jnp.minimum(line + 2, SEQS - 1), logits_even, peak_even)
        weigh(line + 1, logits_odd, peak_odd, taken_odd, total_odd)
        finish(line, taken_even, total_even)
        return carry

    taken_odd[...] = jnp.zeros((256, LANES), BF16)
    total_odd[...] = jnp.ones((256, LANES), F32)
    lax.fori_loop(0, SEQS // 2, two_lines, 0)
    finish(SEQS - 1, taken_odd, total_odd)

    exits = tile_rows(exit_ref[...], 0)
    update = jnp.zeros(flat, F32)
    for side in range(2):
        exit_side = jnp.where((row >= 64) & (lane // 64 == side), exits, 0.0).astype(BF16)
        update += dot(gateds[:, side * 16 : side * 16 + 16, :].reshape(flat), exit_side)
    line = (lines[...].reshape(flat) + update).astype(BF16)
    normed = normalize(line, 64).astype(BF16)

    def share(buffer, send, recv, d):
        return pltpu.make_async_remote_copy(
            src_ref=buffer.at[0],
            dst_ref=buffer.at[8 - d],
            send_sem=send.at[d],
            recv_sem=recv.at[8 - d],
            device_id=(seq_peers[d - 1], res),
            device_id_type=MESH,
        )

    kept = kepts[...]
    means[0] = jnp.sum(kept * normed.astype(F32).reshape(whole), axis=0).astype(BF16)
    for d in range(1, 8):
        share(means, mean_send, mean_recv, d).start()

    weights = column_ref[...]
    gate = jax.nn.sigmoid(dot(normed, twice(weights, 64)))
    pick_shape = (weights.shape[1], LANES)
    source, at = rows_of(pick_shape), lanes_of(pick_shape)
    tall = dot(flag(row[:, :64] % 64 == lane[:, :64]), weights).astype(BF16)
    same = row // 64 == lane // 64
    key_weights = jnp.where(same, dot(tall, flag(source == 128 + at % 8)), 0.0).astype(BF16)
    value_weights = jnp.where(same, dot(tall, flag(source == 136 + at % 8)), 0.0).astype(BF16)
    query_weights = twice(weights, 0)
    key = dot(normed, key_weights).reshape(whole)
    value = dot(normed, value_weights).reshape(whole)
    head_sum = flag(row // 8 == lane // 8)

    count = jnp.sum(biases[:, 256:272, :].astype(F32), axis=0)
    for d in range(1, 8):
        share(means, mean_send, mean_recv, d).wait_recv()
    mean = jnp.sum(means[...].astype(F32), axis=0) / jnp.maximum(count, 1.0)
    mean_query = dot_split(mean, query_weights) * 8**-0.5
    logits = dot_split((key * mean_query[None]).reshape(flat), head_sum).reshape(whole)
    logits = logits + 1000000000.0 * (kept - 1.0)
    peak = jnp.max(logits, axis=0)
    exped = jnp.exp(logits - peak[None])
    total = jnp.sum(exped, axis=0)
    sums[0, 0:16, :] = (jnp.sum(exped * value, axis=0) / total).astype(BF16)
    weight = peak + jnp.log(total)
    part = lanes_of((PAIRS, LANES)) % 8
    terms = jnp.zeros((PAIRS, LANES), BF16)
    for term in range(3):
        rounded = weight.astype(BF16)
        terms = jnp.where(part == term, rounded.astype(F32), terms.astype(F32)).astype(BF16)
        weight = weight - rounded.astype(F32)
    sums[0, 16:32, :] = terms
    for d in range(1, 8):
        share(sums, sum_send, sum_recv, d).start()
    for d in range(1, 8):
        share(sums, sum_send, sum_recv, d).wait_recv()
    weight = dot(sums[:, 16:32, :].reshape(8 * PAIRS, LANES), head_sum).reshape(8, PAIRS, LANES)
    factor = jnp.exp(weight - jnp.max(weight, axis=0)[None])
    attended = jnp.sum(factor * sums[:, 0:16, :].astype(F32), axis=0) / jnp.sum(factor, axis=0)
    gated = (gate.reshape(whole) * attended[None]).astype(BF16).reshape(flat)
    final = line.astype(F32) + dot(gated, twice(exit_col_ref[...], 0))
    results[...] = final.reshape(whole)
    for tile in range(PAIRS):
        out_ref[:, tile * LANES : (tile + 1) * LANES] = results[:, tile, :].astype(BF16)

    for slot in range(7):
        bias_copy(seq, slot, seq).wait_send()
    for d in range(1, 8):
        share(means, mean_send, mean_recv, d).wait_send()
        share(sums, sum_send, sum_recv, d).wait_send()
    for side, source in enumerate((y, y, y, core)):
        own_copy(side, source).wait_send()
    for group in range(GROUPS):
        for d in (1, 2, 3):
            z_copy(group, d).wait_send()
        for side in range(3):
            y_copy(group, side, y).wait_send()
        for slot in range(4):
            core_copy(group, slot, y, core).wait_send()


def on_device(
    extra_activations,
    twofold_representation,
    present_indicator,
    amino_presence,
    twofold_offset_matrix,
    horizontal_matrix,
    horizontal_exit_matrix,
    vertical_matrix,
    vertical_exit_matrix,
):
    operands = [
        extra_activations,
        twofold_representation,
        present_indicator,
        amino_presence.reshape(1, RES),
        twofold_offset_matrix.T,
        horizontal_matrix,
        horizontal_exit_matrix,
        vertical_matrix,
        vertical_exit_matrix,
    ]
    dma, vmem = pltpu.SemaphoreType.DMA, pltpu.VMEM
    return pl.pallas_call(
        fused_kernel,
        out_shape=jax.ShapeDtypeStruct((SEQS, RES * 64), BF16),
        in_specs=[pl.BlockSpec(memory_space=pltpu.HBM)] * len(operands),
        out_specs=pl.BlockSpec(memory_space=vmem),
        scratch_shapes=[vmem(operand.shape, operand.dtype) for operand in operands]
        + [
            vmem((4, 4, 2, ROWS, LANES), BF16),
            vmem((8, 272, LANES), BF16),
            vmem((SEQS, PAIRS, LANES), F32),
            vmem((256, LANES), F32),
            vmem((512, 512), F32),
            vmem((SEQS, 512, LANES), BF16),
            vmem((SEQS, 32, LANES), F32),
            vmem((SEQS, 32, LANES), BF16),
            vmem((512, 512), F32),
            vmem((512, 512), F32),
            vmem((256, LANES), F32),
            vmem((256, LANES), F32),
            vmem((256, LANES), BF16),
            vmem((256, LANES), BF16),
            vmem((256, LANES), F32),
            vmem((256, LANES), F32),
            vmem((SEQS, PAIRS, LANES), F32),
            vmem((SEQS, PAIRS, LANES), F32),
            vmem((8, PAIRS, LANES), BF16),
            vmem((8, 32, LANES), BF16),
            dma((len(operands),)),
            dma((GROUPS, 10)),
            dma((4,)),
            dma((4,)),
            dma((4, GROUPS)),
            dma((3, GROUPS)),
            dma((4, GROUPS)),
            dma((7,)),
            dma((8,)),
            dma((8,)),
            dma((8,)),
            dma((8,)),
            dma((8,)),
        ],
        compiler_params=pltpu.CompilerParams(
            collective_id=0, has_side_effects=True, vmem_limit_bytes=60 << 20
        ),
        name="fused",
    )(*operands)


def solution(mesh):
    in_specs = (
        P("seq", "res"),
        P("res", "seq", None),
        P("seq", "res"),
        P("res"),
        P(),
        P(),
        P(),
        P(),
        P(),
    )
    out_specs = P("seq", "res")
    return jax.shard_map(
        on_device, mesh=mesh, in_specs=in_specs, out_specs=out_specs, check_vma=False
    )
```

```python
import jax
import jax.numpy as jnp
from jax import lax
from jax.experimental import pallas as pl
from jax.experimental.pallas import tpu as pltpu
from jax.sharding import PartitionSpec as P

MESH = pl.DeviceIdType.MESH
F32, BF16 = jnp.float32, jnp.bfloat16
SEQS, RES, PAIRS, LANES = 32, 32, 16, 128
ROWS = PAIRS + SEQS * PAIRS
COUNTS = (4, 8, 10, 10)
GROUPS = len(COUNTS)
LOG2E = 1.4426950408889634
SPANS = [
    (0 if g == 0 else PAIRS * (1 + sum(COUNTS[:g])), PAIRS * (COUNTS[g] + (g == 0)))
    for g in range(GROUPS)
]


def rows_of(shape):
    return lax.broadcasted_iota(jnp.int32, shape, 0)


def lanes_of(shape):
    return lax.broadcasted_iota(jnp.int32, shape, 1)


def flag(condition):
    return jnp.where(condition, 1.0, 0.0).astype(BF16)


def dot(left, right):
    return jnp.dot(left, right, preferred_element_type=F32)


def dot_nt(left, right):
    return lax.dot_general(left, right, (((1,), (1,)), ((), ())), preferred_element_type=F32)


def dot_split(left, right):
    high = left.astype(BF16)
    low = (left - high.astype(F32)).astype(BF16)
    return dot(high, right) + dot(low, right)


def normalize(values, width):
    shape = (LANES, LANES)
    average = jnp.where(
        rows_of(shape) // width == lanes_of(shape) // width, 1.0 / width, 0.0
    ).astype(BF16)
    centre = values.astype(F32) - dot(values, average)
    squares = centre * centre
    spread = dot_split(squares, average)
    return centre * lax.rsqrt(spread + 1e-05)


def tile_rows(weights, shift):
    height, width = weights.shape
    tall = dot(flag(rows_of((LANES, height)) % height == lanes_of((LANES, height))), weights)
    column = rows_of((width, LANES))
    pick = flag(column == lanes_of((width, LANES)) % 64 + shift)
    return dot(tall.astype(BF16), pick)


def twice(weights, shift):
    shape = (LANES, LANES)
    return jnp.where(
        rows_of(shape) // 64 == lanes_of(shape) // 64, tile_rows(weights, shift), 0.0
    ).astype(BF16)


SCHEDULE = [
    (1, "core", 1),
    (2, 'near', 3),
    (3, 'next', 2),
    (5, 'core', 2),
    (6, 'next', 3),
    (10, 'core', 3),
]


def fused_kernel(
    x_hbm,
    pair_hbm,
    present_hbm,
    amino_hbm,
    offset_hbm,
    weights_hbm,
    exit_hbm,
    column_hbm,
    exit_col_hbm,
    out_ref,
    x_ref,
    pair_ref,
    present_ref,
    amino_ref,
    offset_ref,
    weights_ref,
    exit_ref,
    column_ref,
    exit_col_ref,
    blocks,
    biases,
    lines,
    offsets,
    bias,
    queries,
    gates,
    gateds,
    logits_even,
    logits_odd,
    peak_even,
    peak_odd,
    taken_even,
    taken_odd,
    total_even,
    total_odd,
    kepts,
    results,
    means,
    sums,
    load_sem,
    send_sem,
    own_send,
    own_recv,
    z_recv,
    y_recv,
    core_recv,
    bias_send,
    bias_recv,
    mean_send,
    mean_recv,
    sum_send,
    sum_recv,
):
    loads = [
        pltpu.make_async_copy(source, target, load_sem.at[slot])
        for slot, (source, target) in enumerate(
            [
                (x_hbm, x_ref),
                (present_hbm, present_ref),
                (amino_hbm, amino_ref),
                (pair_hbm, pair_ref),
                (offset_hbm, offset_ref),
                (weights_hbm, weights_ref),
                (exit_hbm, exit_ref),
                (column_hbm, column_ref),
                (exit_col_hbm, exit_col_ref),
            ]
        )
    ]
    for load in loads:
        load.start()
    seq, res = lax.axis_index("seq"), lax.axis_index("res")
    core, y, z = res % 2, (res // 2) % 4, res // 8
    up, down, across = (y + 1) % 4, (y + 3) % 4, (y + 2) % 4
    partner = seq // 2 * 2 + (1 - seq % 2)
    bias_peers = [partner] + [(seq + 2 * d) % 8 for d in (1, 2, 3)]
    seq_peers = [(seq + d) % 8 for d in range(1, 8)]

    def place(z_at, y_at, core_at):
        return (z_at * 4 + y_at) * 2 + core_at

    z_peers = [place((z + d) % 4, y, core) for d in (1, 2, 3)]
    up_peer, down_peer, core_peer = place(z, up, core), place(z, down, core), place(z, y, 1 - core)
    across_peer = place(z, across, core)
    res_peers = z_peers + [up_peer, down_peer, across_peer, core_peer]
    barrier = pltpu.get_barrier_semaphore()
    for peer in seq_peers:
        pl.semaphore_signal(barrier, inc=1, device_id=(peer, res), device_id_type=MESH)
    for peer in res_peers:
        pl.semaphore_signal(barrier, inc=1, device_id=(seq, peer), device_id_type=MESH)

    whole = (SEQS, PAIRS, LANES)
    flat = (SEQS * PAIRS, LANES)
    for load in loads[0:3]:
        load.wait()
    for tile in range(PAIRS):
        lines[:, tile, :] = x_ref[:, tile * LANES : (tile + 1) * LANES].astype(F32)
    own = normalize(lines[...].reshape(flat).astype(BF16), 64).astype(BF16)
    blocks[0, y, core, PAIRS:ROWS, :] = own
    kept = (present_ref[...] * amino_ref[...]).astype(F32).astype(BF16)
    turned = jnp.zeros((PAIRS, LANES), F32)
    counted = jnp.zeros((PAIRS, LANES), F32)
    for parity in range(2):
        shape = (PAIRS, SEQS)
        picked = dot_nt(flag(lanes_of(shape) == 2 * rows_of(shape) + parity), kept)
        shape = (SEQS, LANES)
        turned += dot(
            picked.astype(BF16), flag(lanes_of(shape) == rows_of(shape) + parity * SEQS)
        )
        counted += dot(picked.astype(BF16), flag(lanes_of(shape) // 64 == parity))
    biases[seq, 256:272, :] = counted.astype(BF16)
    blocks[0, y, core, 0:PAIRS, :] = jnp.where(
        lanes_of((PAIRS, LANES)) < 64, 1000000000.0 * (turned - 1.0), 1.0
    ).astype(BF16)

    def remote(view, send, recv, target):
        return pltpu.make_async_remote_copy(
            src_ref=view,
            dst_ref=view,
            send_sem=send,
            recv_sem=recv,
            device_id=(seq, target),
            device_id_type=MESH,
        )

    def column(y_at, core_at, group, first=0, count=4):
        return blocks.at[pl.ds(first, count), y_at, core_at, pl.ds(*SPANS[group]), :]

    def z_copy(group, d):
        rows = pl.ds(*SPANS[group])
        return pltpu.make_async_remote_copy(
            src_ref=blocks.at[0, y, core, rows, :],
            dst_ref=blocks.at[4 - d, y, core, rows, :],
            send_sem=send_sem.at[group, d - 1],
            recv_sem=z_recv.at[4 - d, group],
            device_id=(seq, z_peers[d - 1]),
            device_id_type=MESH,
        )

    def own_copy(side, source):
        target = (up_peer, down_peer, across_peer, core_peer)[side]
        return remote(
            blocks.at[0, source, core] if side < 3 else blocks.at[0, y, source],
            own_send.at[side],
            own_recv.at[(1, 0, 2, 3)[side]],
            target,
        )

    def y_copy(group, side, source):
        target = (up_peer, down_peer, across_peer)[side]
        return remote(
            column(source, core, group, 1, 3),
            send_sem.at[group, 3 + side],
            y_recv.at[(1, 0, 2)[side], group],
            target,
        )

    def core_copy(group, slot, source, core_at):
        first = 1 if slot == 0 else 0
        return remote(
            column(source, core_at, group, first, 4 - first),
            send_sem.at[group, 6 + slot],
            core_recv.at[slot, group],
            core_peer,
        )

    def stage_near(group):
        for d in (1, 2, 3):
            z_copy(group, d).wait_recv()
        if group + 1 < GROUPS:
            for d in (1, 2, 3):
                z_copy(group + 1, d).start()
        for side in range(3):
            y_copy(group, side, y).start()
        core_copy(group, 0, y, core).start()

    def stage_next(group):
        for side, source in enumerate((down, up, across)):
            if group == 0:
                own_copy(side, source).wait_recv()
            y_copy(group, side, source).wait_recv()
            core_copy(group, side + 1, source, core).start()

    def stage_core(group):
        if group == 0:
            own_copy(3, 1 - core).wait_recv()
        for slot, at in enumerate((y, down, up, across)):
            core_copy(group, slot, at, 1 - core).wait_recv()

    def bias_copy(block, slot, target):
        return pltpu.make_async_remote_copy(
            src_ref=biases.at[block],
            dst_ref=biases.at[block],
            send_sem=bias_send.at[slot],
            recv_sem=bias_recv.at[block],
            device_id=(target, res),
            device_id_type=MESH,
        )

    pl.semaphore_wait(barrier, len(seq_peers) + len(res_peers))
    for side in range(3):
        own_copy(side, y).start()
    for d in (1, 2, 3):
        z_copy(0, d).start()
    own_copy(3, core).start()

    for load in loads[3:5]:
        load.wait()

    shape = (256, 256)
    average = jnp.where(
        rows_of(shape) // LANES == lanes_of(shape) // LANES, 1.0 / LANES, 0.0
    ).astype(BF16)

    def bias_rows(step, carry):
        pair = pair_ref[pl.ds(step * 4, 4)].reshape(4 * LANES, LANES)
        pair = jnp.concatenate([pair[:256], pair[256:]], axis=1)
        centre = pair.astype(F32) - dot(pair, average)
        spread = dot((centre * centre).astype(BF16), average)
        normed = (centre * lax.rsqrt(spread + 1e-05)).astype(BF16)
        for row in range(4):
            start = row // 2 * LANES
            found = dot_nt(
                offset_ref[...],
                normed[row % 2 * LANES : row % 2 * LANES + LANES, start : start + LANES],
            )
            offsets[pl.ds(pl.multiple_of(step * 32 + row * 8, 8), 8), :] = found
        return carry

    lax.fori_loop(0, 8, bias_rows, 0, unroll=2)
    for head in range(8):
        for parity in range(2):
            biases[seq, pl.ds(head * 32 + parity * 16, 16), :] = offsets[
                pl.ds(parity * 8 + head, 16, stride=16), :
            ].astype(BF16)

    for slot, peer in enumerate(bias_peers):
        bias_copy(seq, slot, peer).start()

    for load in loads[5:]:
        load.wait()
    weights = weights_ref[...]
    square = (LANES, LANES)
    row, lane = rows_of(square), lanes_of(square)
    wide = (LANES, 256)
    turned = dot_nt(flag(lanes_of(wide) == rows_of(wide) % 64 + 64), weights).astype(BF16)
    shape = (64, LANES)
    turned = dot(turned, flag(rows_of(shape) == lanes_of(shape) % 64))
    query_weights = tile_rows(weights, 0)
    gate_weights = tile_rows(weights, 192)

    def query_side(side):
        mine = row // 64 == side
        query = dot(own, jnp.where(mine, query_weights, 0.0).astype(BF16))
        query = (query * (LOG2E * 8**-0.5)).astype(BF16)
        gate = dot(own, jnp.where(mine, gate_weights, 0.0).astype(BF16))
        gates[:, side * 16 : side * 16 + 16, :] = jax.nn.sigmoid(gate).reshape(whole)
        for head in range(8):
            keyed = jnp.where(row // 8 == head, turned, 0.0)
            both = jnp.concatenate(
                [jnp.where(lane // 64 == parity, keyed, 0.0) for parity in range(2)], axis=1
            ).astype(BF16)
            found = dot(query, both).astype(BF16)
            for parity in range(2):
                start = (parity * 8 + head) * 32 + side * 16
                queries[:, start : start + 16, :] = found[
                    :, parity * LANES : (parity + 1) * LANES
                ].reshape(whole)

    stage_near(0)
    query_side(0)
    query_side(1)
    stage_next(0)
    bias_copy(partner, 0, seq).wait_recv()
    for slot, peer in enumerate(bias_peers[1:]):
        bias_copy(partner, 4 + slot, peer).start()
    stage_near(1)

    spread = (RES, RES * 64)
    kept = dot(kept, flag(rows_of(spread) == lanes_of(spread) // 64))
    for tile in range(PAIRS):
        kepts[:, tile, :] = kept[:, tile * LANES : (tile + 1) * LANES]

    for peer in bias_peers[1:]:
        bias_copy(peer, 0, seq).wait_recv()
        bias_copy(peer // 2 * 2 + (1 - peer % 2), 0, seq).wait_recv()
    shape = (256, 256)
    order = flag(rows_of(shape) == 2 * (lanes_of(shape) % LANES) + lanes_of(shape) // LANES)
    for tile in range(4):
        at = (z + tile) % 4
        both = jnp.concatenate([biases[2 * at, 0:256], biases[2 * at + 1, 0:256]], axis=1)
        placed = dot(both, order) * LOG2E
        for parity in range(2):
            bias[parity * 256 : parity * 256 + 256, tile * LANES : (tile + 1) * LANES] = placed[
                :, parity * LANES : (parity + 1) * LANES
            ]
    stage_core(0)
    stage_next(1)
    stage_near(2)

    value_weights = jnp.where(lane >= 64, tile_rows(weights, 128), 0.0).astype(BF16)
    half = lanes_of((256, LANES)) < 64
    head_of = lanes_of((32, LANES)) // 8 - 8

    def keys_of(line):
        start = pl.multiple_of(PAIRS + line * PAIRS, PAIRS)
        keys = blocks[:, :, :, pl.ds(start, PAIRS), :].reshape(512, LANES)
        mask = blocks[:, :, :, 0:PAIRS, :].reshape(512, LANES)
        return jnp.concatenate([keys, mask], axis=1)

    def score(line, logits_ref, peak_ref):
        at = lanes_of((PAIRS, LANES))
        picks = [flag(at == line)] * 16 + [flag(at == line + SEQS)] * 16
        left = jnp.concatenate([queries[line], jnp.concatenate(picks, axis=0)], axis=1)
        logits = dot_nt(left, keys_of(line)) + bias[...]
        logits_ref[...] = logits
        peak = jnp.maximum(
            jnp.maximum(logits[:, 0:128], logits[:, 128:256]),
            jnp.maximum(logits[:, 256:384], logits[:, 384:512]),
        )
        peak = jnp.max(jnp.maximum(peak[:256], peak[256:]), axis=1, keepdims=True)
        peak_ref[...] = jnp.broadcast_to(peak, (256, LANES))

    def weigh(line, logits_ref, peak_ref, taken_ref, total_ref):
        peak = jnp.concatenate([peak_ref[...]] * 4, axis=1)
        peak = jnp.concatenate([peak, peak], axis=0)
        exped = jnp.exp2(logits_ref[...] - peak).astype(BF16)
        summed = dot(exped, keys_of(line))
        taken_ref[...] = jnp.where(half, summed[:256, :LANES], summed[256:, :LANES]).astype(BF16)
        total_ref[...] = summed[:256, LANES:] + summed[256:, LANES:]

    def finish(line, taken_ref, total_ref):
        found = dot(taken_ref[...], value_weights) / total_ref[...]
        attended = jnp.zeros((32, LANES), F32)
        for head in range(8):
            attended = jnp.where(head_of == head, found[head * 32 : head * 32 + 32], attended)
        gateds[line] = (gates[line] * attended).astype(BF16)

    stages = {"near": stage_near, "next": stage_next, "core": stage_core}
    score(0, logits_even, peak_even)

    def two_lines(step, carry):
        for at, stage, group in SCHEDULE:

            @pl.when(step == at)
            def _():
                stages[stage](group)

        line = 2 * step
        score(line + 1, logits_odd, peak_odd)
        weigh(line, logits_even, peak_even, taken_even, total_even)
        finish(jnp.maximum(line - 1, 0), taken_odd, total_odd)
        score(jnp.minimum(line + 2, SEQS - 1), logits_even, peak_even)
        weigh(line + 1, logits_odd, peak_odd, taken_odd, total_odd)
        finish(line, taken_even, total_even)
        return carry

    taken_odd[...] = jnp.zeros((256, LANES), BF16)
    total_odd[...] = jnp.ones((256, LANES), F32)
    lax.fori_loop(0, SEQS // 2, two_lines, 0)
    finish(SEQS - 1, taken_odd, total_odd)

    exits = tile_rows(exit_ref[...], 0)
    update = jnp.zeros(flat, F32)
    for side in range(2):
        exit_side = jnp.where((row >= 64) & (lane // 64 == side), exits, 0.0).astype(BF16)
        update += dot(gateds[:, side * 16 : side * 16 + 16, :].reshape(flat), exit_side)
    line = (lines[...].reshape(flat) + update).astype(BF16)
    normed = normalize(line, 64).astype(BF16)

    def share(buffer, send, recv, d):
        return pltpu.make_async_remote_copy(
            src_ref=buffer.at[0],
            dst_ref=buffer.at[8 - d],
            send_sem=send.at[d],
            recv_sem=recv.at[8 - d],
            device_id=(seq_peers[d - 1], res),
            device_id_type=MESH,
        )

    kept = kepts[...]
    means[0] = jnp.sum(kept * normed.astype(F32).reshape(whole), axis=0).astype(BF16)
    for d in range(1, 8):
        share(means, mean_send, mean_recv, d).start()

    weights = column_ref[...]
    gate = jax.nn.sigmoid(dot(normed, twice(weights, 64)))
    pick_shape = (weights.shape[1], LANES)
    source, at = rows_of(pick_shape), lanes_of(pick_shape)
    tall = dot(flag(row[:, :64] % 64 == lane[:, :64]), weights).astype(BF16)
    same = row // 64 == lane // 64
    key_weights = jnp.where(same, dot(tall, flag(source == 128 + at % 8)), 0.0).astype(BF16)
    value_weights = jnp.where(same, dot(tall, flag(source == 136 + at % 8)), 0.0).astype(BF16)
    query_weights = twice(weights, 0)
    key = dot(normed, key_weights).reshape(whole)
    value = dot(normed, value_weights).reshape(whole)
    head_sum = flag(row // 8 == lane // 8)

    count = jnp.sum(biases[:, 256:272, :].astype(F32), axis=0)
    for d in range(1, 8):
        share(means, mean_send, mean_recv, d).wait_recv()
    mean = jnp.sum(means[...].astype(F32), axis=0) / jnp.maximum(count, 1.0)
    mean_query = dot_split(mean, query_weights) * 8**-0.5
    logits = dot_split((key * mean_query[None]).reshape(flat), head_sum).reshape(whole)
    logits = logits + 1000000000.0 * (kept - 1.0)
    peak = jnp.max(logits, axis=0)
    exped = jnp.exp(logits - peak[None])
    total = jnp.sum(exped, axis=0)
    sums[0, 0:16, :] = (jnp.sum(exped * value, axis=0) / total).astype(BF16)
    weight = peak + jnp.log(total)
    part = lanes_of((PAIRS, LANES)) % 8
    terms = jnp.zeros((PAIRS, LANES), BF16)
    for term in range(3):
        rounded = weight.astype(BF16)
        terms = jnp.where(part == term, rounded.astype(F32), terms.astype(F32)).astype(BF16)
        weight = weight - rounded.astype(F32)
    sums[0, 16:32, :] = terms
    for d in range(1, 8):
        share(sums, sum_send, sum_recv, d).start()
    for d in range(1, 8):
        share(sums, sum_send, sum_recv, d).wait_recv()
    weight = dot(sums[:, 16:32, :].reshape(8 * PAIRS, LANES), head_sum).reshape(8, PAIRS, LANES)
    factor = jnp.exp(weight - jnp.max(weight, axis=0)[None])
    attended = jnp.sum(factor * sums[:, 0:16, :].astype(F32), axis=0) / jnp.sum(factor, axis=0)
    gated = (gate.reshape(whole) * attended[None]).astype(BF16).reshape(flat)
    final = line.astype(F32) + dot(gated, twice(exit_col_ref[...], 0))
    results[...] = final.reshape(whole)
    for tile in range(PAIRS):
        out_ref[:, tile * LANES : (tile + 1) * LANES] = results[:, tile, :].astype(BF16)

    for slot in range(7):
        bias_copy(seq, slot, seq).wait_send()
    for d in range(1, 8):
        share(means, mean_send, mean_recv, d).wait_send()
        share(sums, sum_send, sum_recv, d).wait_send()
    for side, source in enumerate((y, y, y, core)):
        own_copy(side, source).wait_send()
    for group in range(GROUPS):
        for d in (1, 2, 3):
            z_copy(group, d).wait_send()
        for side in range(3):
            y_copy(group, side, y).wait_send()
        for slot in range(4):
            core_copy(group, slot, y, core).wait_send()


def on_device(
    extra_activations,
    twofold_representation,
    present_indicator,
    amino_presence,
    twofold_offset_matrix,
    horizontal_matrix,
    horizontal_exit_matrix,
    vertical_matrix,
    vertical_exit_matrix,
):
    operands = [
        extra_activations,
        twofold_representation,
        present_indicator,
        amino_presence.reshape(1, RES),
        twofold_offset_matrix.T,
        horizontal_matrix,
        horizontal_exit_matrix,
        vertical_matrix,
        vertical_exit_matrix,
    ]
    dma, vmem = pltpu.SemaphoreType.DMA, pltpu.VMEM
    return pl.pallas_call(
        fused_kernel,
        out_shape=jax.ShapeDtypeStruct((SEQS, RES * 64), BF16),
        in_specs=[pl.BlockSpec(memory_space=pltpu.HBM)] * len(operands),
        out_specs=pl.BlockSpec(memory_space=vmem),
        scratch_shapes=[vmem(operand.shape, operand.dtype) for operand in operands]
        + [
            vmem((4, 4, 2, ROWS, LANES), BF16),
            vmem((8, 272, LANES), BF16),
            vmem((SEQS, PAIRS, LANES), F32),
            vmem((256, LANES), F32),
            vmem((512, 512), F32),
            vmem((SEQS, 512, LANES), BF16),
            vmem((SEQS, 32, LANES), F32),
            vmem((SEQS, 32, LANES), BF16),
            vmem((512, 512), F32),
            vmem((512, 512), F32),
            vmem((256, LANES), F32),
            vmem((256, LANES), F32),
            vmem((256, LANES), BF16),
            vmem((256, LANES), BF16),
            vmem((256, LANES), F32),
            vmem((256, LANES), F32),
            vmem((SEQS, PAIRS, LANES), F32),
            vmem((SEQS, PAIRS, LANES), F32),
            vmem((8, PAIRS, LANES), BF16),
            vmem((8, 32, LANES), BF16),
            dma((len(operands),)),
            dma((GROUPS, 10)),
            dma((4,)),
            dma((4,)),
            dma((4, GROUPS)),
            dma((3, GROUPS)),
            dma((4, GROUPS)),
            dma((7,)),
            dma((8,)),
            dma((8,)),
            dma((8,)),
            dma((8,)),
            dma((8,)),
        ],
        compiler_params=pltpu.CompilerParams(
            collective_id=0, has_side_effects=True, vmem_limit_bytes=60 << 20
        ),
        name="fused",
    )(*operands)


def solution(mesh):
    in_specs = (
        P("seq", "res"),
        P("res", "seq", None),
        P("seq", "res"),
        P("res"),
        P(),
        P(),
        P(),
        P(),
        P(),
    )
    out_specs = P("seq", "res")
    return jax.shard_map(
        on_device, mesh=mesh, in_specs=in_specs, out_specs=out_specs, check_vma=False
    )
```

```python
import jax
import jax.numpy as jnp
from jax import lax
from jax.experimental import pallas as pl
from jax.experimental.pallas import tpu as pltpu
from jax.sharding import PartitionSpec as P

MESH = pl.DeviceIdType.MESH
F32, BF16 = jnp.float32, jnp.bfloat16
SEQS, RES, PAIRS, LANES = 32, 32, 16, 128
ROWS = PAIRS + SEQS * PAIRS
COUNTS = (4, 8, 12, 8)
GROUPS = len(COUNTS)
LOG2E = 1.4426950408889634
SPANS = [
    (0 if g == 0 else PAIRS * (1 + sum(COUNTS[:g])), PAIRS * (COUNTS[g] + (g == 0)))
    for g in range(GROUPS)
]


def rows_of(shape):
    return lax.broadcasted_iota(jnp.int32, shape, 0)


def lanes_of(shape):
    return lax.broadcasted_iota(jnp.int32, shape, 1)


def flag(condition):
    return jnp.where(condition, 1.0, 0.0).astype(BF16)


def dot(left, right):
    return jnp.dot(left, right, preferred_element_type=F32)


def dot_nt(left, right):
    return lax.dot_general(left, right, (((1,), (1,)), ((), ())), preferred_element_type=F32)


def dot_split(left, right):
    high = left.astype(BF16)
    low = (left - high.astype(F32)).astype(BF16)
    return dot(high, right) + dot(low, right)


def normalize(values, width):
    shape = (LANES, LANES)
    average = jnp.where(
        rows_of(shape) // width == lanes_of(shape) // width, 1.0 / width, 0.0
    ).astype(BF16)
    centre = values.astype(F32) - dot(values, average)
    squares = centre * centre
    spread = dot_split(squares, average)
    return centre * lax.rsqrt(spread + 1e-05)


def tile_rows(weights, shift):
    height, width = weights.shape
    tall = dot(flag(rows_of((LANES, height)) % height == lanes_of((LANES, height))), weights)
    column = rows_of((width, LANES))
    pick = flag(column == lanes_of((width, LANES)) % 64 + shift)
    return dot(tall.astype(BF16), pick)


def twice(weights, shift):
    shape = (LANES, LANES)
    return jnp.where(
        rows_of(shape) // 64 == lanes_of(shape) // 64, tile_rows(weights, shift), 0.0
    ).astype(BF16)


SCHEDULE = [
    (1, "core", 1),
    (2, 'near', 3),
    (3, 'next', 2),
    (5, 'core', 2),
    (6, 'next', 3),
    (11, "core", 3),
]


def fused_kernel(
    x_hbm,
    pair_hbm,
    present_hbm,
    amino_hbm,
    offset_hbm,
    weights_hbm,
    exit_hbm,
    column_hbm,
    exit_col_hbm,
    out_ref,
    x_ref,
    pair_ref,
    present_ref,
    amino_ref,
    offset_ref,
    weights_ref,
    exit_ref,
    column_ref,
    exit_col_ref,
    blocks,
    biases,
    lines,
    offsets,
    bias,
    queries,
    gates,
    gateds,
    logits_even,
    logits_odd,
    peak_even,
    peak_odd,
    taken_even,
    taken_odd,
    total_even,
    total_odd,
    kepts,
    results,
    means,
    sums,
    load_sem,
    send_sem,
    own_send,
    own_recv,
    z_recv,
    y_recv,
    core_recv,
    bias_send,
    bias_recv,
    mean_send,
    mean_recv,
    sum_send,
    sum_recv,
):
    loads = [
        pltpu.make_async_copy(source, target, load_sem.at[slot])
        for slot, (source, target) in enumerate(
            [
                (x_hbm, x_ref),
                (present_hbm, present_ref),
                (amino_hbm, amino_ref),
                (pair_hbm, pair_ref),
                (offset_hbm, offset_ref),
                (weights_hbm, weights_ref),
                (exit_hbm, exit_ref),
                (column_hbm, column_ref),
                (exit_col_hbm, exit_col_ref),
            ]
        )
    ]
    for load in loads:
        load.start()
    seq, res = lax.axis_index("seq"), lax.axis_index("res")
    core, y, z = res % 2, (res // 2) % 4, res // 8
    up, down, across = (y + 1) % 4, (y + 3) % 4, (y + 2) % 4
    partner = seq // 2 * 2 + (1 - seq % 2)
    bias_peers = [partner] + [(seq + 2 * d) % 8 for d in (1, 2, 3)]
    seq_peers = [(seq + d) % 8 for d in range(1, 8)]

    def place(z_at, y_at, core_at):
        return (z_at * 4 + y_at) * 2 + core_at

    z_peers = [place((z + d) % 4, y, core) for d in (1, 2, 3)]
    up_peer, down_peer, core_peer = place(z, up, core), place(z, down, core), place(z, y, 1 - core)
    across_peer = place(z, across, core)
    res_peers = z_peers + [up_peer, down_peer, across_peer, core_peer]
    barrier = pltpu.get_barrier_semaphore()
    for peer in seq_peers:
        pl.semaphore_signal(barrier, inc=1, device_id=(peer, res), device_id_type=MESH)
    for peer in res_peers:
        pl.semaphore_signal(barrier, inc=1, device_id=(seq, peer), device_id_type=MESH)

    whole = (SEQS, PAIRS, LANES)
    flat = (SEQS * PAIRS, LANES)
    for load in loads[0:3]:
        load.wait()
    for tile in range(PAIRS):
        lines[:, tile, :] = x_ref[:, tile * LANES : (tile + 1) * LANES].astype(F32)
    own = normalize(lines[...].reshape(flat).astype(BF16), 64).astype(BF16)
    blocks[0, y, core, PAIRS:ROWS, :] = own
    kept = (present_ref[...] * amino_ref[...]).astype(F32).astype(BF16)
    turned = jnp.zeros((PAIRS, LANES), F32)
    counted = jnp.zeros((PAIRS, LANES), F32)
    for parity in range(2):
        shape = (PAIRS, SEQS)
        picked = dot_nt(flag(lanes_of(shape) == 2 * rows_of(shape) + parity), kept)
        shape = (SEQS, LANES)
        turned += dot(
            picked.astype(BF16), flag(lanes_of(shape) == rows_of(shape) + parity * SEQS)
        )
        counted += dot(picked.astype(BF16), flag(lanes_of(shape) // 64 == parity))
    biases[seq, 256:272, :] = counted.astype(BF16)
    blocks[0, y, core, 0:PAIRS, :] = jnp.where(
        lanes_of((PAIRS, LANES)) < 64, 1000000000.0 * (turned - 1.0), 1.0
    ).astype(BF16)

    def remote(view, send, recv, target):
        return pltpu.make_async_remote_copy(
            src_ref=view,
            dst_ref=view,
            send_sem=send,
            recv_sem=recv,
            device_id=(seq, target),
            device_id_type=MESH,
        )

    def column(y_at, core_at, group, first=0, count=4):
        return blocks.at[pl.ds(first, count), y_at, core_at, pl.ds(*SPANS[group]), :]

    def z_copy(group, d):
        rows = pl.ds(*SPANS[group])
        return pltpu.make_async_remote_copy(
            src_ref=blocks.at[0, y, core, rows, :],
            dst_ref=blocks.at[4 - d, y, core, rows, :],
            send_sem=send_sem.at[group, d - 1],
            recv_sem=z_recv.at[4 - d, group],
            device_id=(seq, z_peers[d - 1]),
            device_id_type=MESH,
        )

    def own_copy(side, source):
        target = (up_peer, down_peer, across_peer, core_peer)[side]
        return remote(
            blocks.at[0, source, core] if side < 3 else blocks.at[0, y, source],
            own_send.at[side],
            own_recv.at[(1, 0, 2, 3)[side]],
            target,
        )

    def y_copy(group, side, source):
        target = (up_peer, down_peer, across_peer)[side]
        return remote(
            column(source, core, group, 1, 3),
            send_sem.at[group, 3 + side],
            y_recv.at[(1, 0, 2)[side], group],
            target,
        )

    def core_copy(group, slot, source, core_at):
        first = 1 if slot == 0 else 0
        return remote(
            column(source, core_at, group, first, 4 - first),
            send_sem.at[group, 6 + slot],
            core_recv.at[slot, group],
            core_peer,
        )

    def stage_near(group):
        for d in (1, 2, 3):
            z_copy(group, d).wait_recv()
        if group + 1 < GROUPS:
            for d in (1, 2, 3):
                z_copy(group + 1, d).start()
        for side in range(3):
            y_copy(group, side, y).start()
        core_copy(group, 0, y, core).start()

    def stage_next(group):
        for side, source in enumerate((down, up, across)):
            if group == 0:
                own_copy(side, source).wait_recv()
            y_copy(group, side, source).wait_recv()
            core_copy(group, side + 1, source, core).start()

    def stage_core(group):
        if group == 0:
            own_copy(3, 1 - core).wait_recv()
        for slot, at in enumerate((y, down, up, across)):
            core_copy(group, slot, at, 1 - core).wait_recv()

    def bias_copy(block, slot, target):
        return pltpu.make_async_remote_copy(
            src_ref=biases.at[block],
            dst_ref=biases.at[block],
            send_sem=bias_send.at[slot],
            recv_sem=bias_recv.at[block],
            device_id=(target, res),
            device_id_type=MESH,
        )

    pl.semaphore_wait(barrier, len(seq_peers) + len(res_peers))
    for side in range(3):
        own_copy(side, y).start()
    for d in (1, 2, 3):
        z_copy(0, d).start()
    own_copy(3, core).start()

    for load in loads[3:5]:
        load.wait()

    shape = (256, 256)
    average = jnp.where(
        rows_of(shape) // LANES == lanes_of(shape) // LANES, 1.0 / LANES, 0.0
    ).astype(BF16)

    def bias_rows(step, carry):
        pair = pair_ref[pl.ds(step * 4, 4)].reshape(4 * LANES, LANES)
        pair = jnp.concatenate([pair[:256], pair[256:]], axis=1)
        centre = pair.astype(F32) - dot(pair, average)
        spread = dot((centre * centre).astype(BF16), average)
        normed = (centre * lax.rsqrt(spread + 1e-05)).astype(BF16)
        for row in range(4):
            start = row // 2 * LANES
            found = dot_nt(
                offset_ref[...],
                normed[row % 2 * LANES : row % 2 * LANES + LANES, start : start + LANES],
            )
            offsets[pl.ds(pl.multiple_of(step * 32 + row * 8, 8), 8), :] = found
        return carry

    lax.fori_loop(0, 8, bias_rows, 0, unroll=2)
    for head in range(8):
        for parity in range(2):
            biases[seq, pl.ds(head * 32 + parity * 16, 16), :] = offsets[
                pl.ds(parity * 8 + head, 16, stride=16), :
            ].astype(BF16)

    for slot, peer in enumerate(bias_peers):
        bias_copy(seq, slot, peer).start()

    for load in loads[5:]:
        load.wait()
    weights = weights_ref[...]
    square = (LANES, LANES)
    row, lane = rows_of(square), lanes_of(square)
    wide = (LANES, 256)
    turned = dot_nt(flag(lanes_of(wide) == rows_of(wide) % 64 + 64), weights).astype(BF16)
    shape = (64, LANES)
    turned = dot(turned, flag(rows_of(shape) == lanes_of(shape) % 64))
    query_weights = tile_rows(weights, 0)
    gate_weights = tile_rows(weights, 192)

    def query_side(side):
        mine = row // 64 == side
        query = dot(own, jnp.where(mine, query_weights, 0.0).astype(BF16))
        query = (query * (LOG2E * 8**-0.5)).astype(BF16)
        gate = dot(own, jnp.where(mine, gate_weights, 0.0).astype(BF16))
        gates[:, side * 16 : side * 16 + 16, :] = jax.nn.sigmoid(gate).reshape(whole)
        for head in range(8):
            keyed = jnp.where(row // 8 == head, turned, 0.0)
            both = jnp.concatenate(
                [jnp.where(lane // 64 == parity, keyed, 0.0) for parity in range(2)], axis=1
            ).astype(BF16)
            found = dot(query, both).astype(BF16)
            for parity in range(2):
                start = (parity * 8 + head) * 32 + side * 16
                queries[:, start : start + 16, :] = found[
                    :, parity * LANES : (parity + 1) * LANES
                ].reshape(whole)

    stage_near(0)
    query_side(0)
    query_side(1)
    stage_next(0)
    bias_copy(partner, 0, seq).wait_recv()
    for slot, peer in enumerate(bias_peers[1:]):
        bias_copy(partner, 4 + slot, peer).start()
    stage_near(1)

    spread = (RES, RES * 64)
    kept = dot(kept, flag(rows_of(spread) == lanes_of(spread) // 64))
    for tile in range(PAIRS):
        kepts[:, tile, :] = kept[:, tile * LANES : (tile + 1) * LANES]

    for peer in bias_peers[1:]:
        bias_copy(peer, 0, seq).wait_recv()
        bias_copy(peer // 2 * 2 + (1 - peer % 2), 0, seq).wait_recv()
    shape = (256, 256)
    order = flag(rows_of(shape) == 2 * (lanes_of(shape) % LANES) + lanes_of(shape) // LANES)
    for tile in range(4):
        at = (z + tile) % 4
        both = jnp.concatenate([biases[2 * at, 0:256], biases[2 * at + 1, 0:256]], axis=1)
        placed = dot(both, order) * LOG2E
        for parity in range(2):
            bias[parity * 256 : parity * 256 + 256, tile * LANES : (tile + 1) * LANES] = placed[
                :, parity * LANES : (parity + 1) * LANES
            ]
    stage_core(0)
    stage_next(1)
    stage_near(2)

    value_weights = jnp.where(lane >= 64, tile_rows(weights, 128), 0.0).astype(BF16)
    half = lanes_of((256, LANES)) < 64
    head_of = lanes_of((32, LANES)) // 8 - 8

    def keys_of(line):
        start = pl.multiple_of(PAIRS + line * PAIRS, PAIRS)
        keys = blocks[:, :, :, pl.ds(start, PAIRS), :].reshape(512, LANES)
        mask = blocks[:, :, :, 0:PAIRS, :].reshape(512, LANES)
        return jnp.concatenate([keys, mask], axis=1)

    def score(line, logits_ref, peak_ref):
        at = lanes_of((PAIRS, LANES))
        picks = [flag(at == line)] * 16 + [flag(at == line + SEQS)] * 16
        left = jnp.concatenate([queries[line], jnp.concatenate(picks, axis=0)], axis=1)
        logits = dot_nt(left, keys_of(line)) + bias[...]
        logits_ref[...] = logits
        peak = jnp.maximum(
            jnp.maximum(logits[:, 0:128], logits[:, 128:256]),
            jnp.maximum(logits[:, 256:384], logits[:, 384:512]),
        )
        peak = jnp.max(jnp.maximum(peak[:256], peak[256:]), axis=1, keepdims=True)
        peak_ref[...] = jnp.broadcast_to(peak, (256, LANES))

    def weigh(line, logits_ref, peak_ref, taken_ref, total_ref):
        peak = jnp.concatenate([peak_ref[...]] * 4, axis=1)
        peak = jnp.concatenate([peak, peak], axis=0)
        exped = jnp.exp2(logits_ref[...] - peak).astype(BF16)
        summed = dot(exped, keys_of(line))
        taken_ref[...] = jnp.where(half, summed[:256, :LANES], summed[256:, :LANES]).astype(BF16)
        total_ref[...] = summed[:256, LANES:] + summed[256:, LANES:]

    def finish(line, taken_ref, total_ref):
        found = dot(taken_ref[...], value_weights) / total_ref[...]
        attended = jnp.zeros((32, LANES), F32)
        for head in range(8):
            attended = jnp.where(head_of == head, found[head * 32 : head * 32 + 32], attended)
        gateds[line] = (gates[line] * attended).astype(BF16)

    stages = {"near": stage_near, "next": stage_next, "core": stage_core}
    score(0, logits_even, peak_even)

    def two_lines(step, carry):
        for at, stage, group in SCHEDULE:

            @pl.when(step == at)
            def _():
                stages[stage](group)

        line = 2 * step
        score(line + 1, logits_odd, peak_odd)
        weigh(line, logits_even, peak_even, taken_even, total_even)
        finish(jnp.maximum(line - 1, 0), taken_odd, total_odd)
        score(jnp.minimum(line + 2, SEQS - 1), logits_even, peak_even)
        weigh(line + 1, logits_odd, peak_odd, taken_odd, total_odd)
        finish(line, taken_even, total_even)
        return carry

    taken_odd[...] = jnp.zeros((256, LANES), BF16)
    total_odd[...] = jnp.ones((256, LANES), F32)
    lax.fori_loop(0, SEQS // 2, two_lines, 0)
    finish(SEQS - 1, taken_odd, total_odd)

    exits = tile_rows(exit_ref[...], 0)
    update = jnp.zeros(flat, F32)
    for side in range(2):
        exit_side = jnp.where((row >= 64) & (lane // 64 == side), exits, 0.0).astype(BF16)
        update += dot(gateds[:, side * 16 : side * 16 + 16, :].reshape(flat), exit_side)
    line = (lines[...].reshape(flat) + update).astype(BF16)
    normed = normalize(line, 64).astype(BF16)

    def share(buffer, send, recv, d):
        return pltpu.make_async_remote_copy(
            src_ref=buffer.at[0],
            dst_ref=buffer.at[8 - d],
            send_sem=send.at[d],
            recv_sem=recv.at[8 - d],
            device_id=(seq_peers[d - 1], res),
            device_id_type=MESH,
        )

    kept = kepts[...]
    means[0] = jnp.sum(kept * normed.astype(F32).reshape(whole), axis=0).astype(BF16)
    for d in range(1, 8):
        share(means, mean_send, mean_recv, d).start()

    weights = column_ref[...]
    gate = jax.nn.sigmoid(dot(normed, twice(weights, 64)))
    pick_shape = (weights.shape[1], LANES)
    source, at = rows_of(pick_shape), lanes_of(pick_shape)
    tall = dot(flag(row[:, :64] % 64 == lane[:, :64]), weights).astype(BF16)
    same = row // 64 == lane // 64
    key_weights = jnp.where(same, dot(tall, flag(source == 128 + at % 8)), 0.0).astype(BF16)
    value_weights = jnp.where(same, dot(tall, flag(source == 136 + at % 8)), 0.0).astype(BF16)
    query_weights = twice(weights, 0)
    key = dot(normed, key_weights).reshape(whole)
    value = dot(normed, value_weights).reshape(whole)
    head_sum = flag(row // 8 == lane // 8)

    count = jnp.sum(biases[:, 256:272, :].astype(F32), axis=0)
    for d in range(1, 8):
        share(means, mean_send, mean_recv, d).wait_recv()
    mean = jnp.sum(means[...].astype(F32), axis=0) / jnp.maximum(count, 1.0)
    mean_query = dot_split(mean, query_weights) * 8**-0.5
    logits = dot_split((key * mean_query[None]).reshape(flat), head_sum).reshape(whole)
    logits = logits + 1000000000.0 * (kept - 1.0)
    peak = jnp.max(logits, axis=0)
    exped = jnp.exp(logits - peak[None])
    total = jnp.sum(exped, axis=0)
    sums[0, 0:16, :] = (jnp.sum(exped * value, axis=0) / total).astype(BF16)
    weight = peak + jnp.log(total)
    part = lanes_of((PAIRS, LANES)) % 8
    terms = jnp.zeros((PAIRS, LANES), BF16)
    for term in range(3):
        rounded = weight.astype(BF16)
        terms = jnp.where(part == term, rounded.astype(F32), terms.astype(F32)).astype(BF16)
        weight = weight - rounded.astype(F32)
    sums[0, 16:32, :] = terms
    for d in range(1, 8):
        share(sums, sum_send, sum_recv, d).start()
    for d in range(1, 8):
        share(sums, sum_send, sum_recv, d).wait_recv()
    weight = dot(sums[:, 16:32, :].reshape(8 * PAIRS, LANES), head_sum).reshape(8, PAIRS, LANES)
    factor = jnp.exp(weight - jnp.max(weight, axis=0)[None])
    attended = jnp.sum(factor * sums[:, 0:16, :].astype(F32), axis=0) / jnp.sum(factor, axis=0)
    gated = (gate.reshape(whole) * attended[None]).astype(BF16).reshape(flat)
    final = line.astype(F32) + dot(gated, twice(exit_col_ref[...], 0))
    results[...] = final.reshape(whole)
    for tile in range(PAIRS):
        out_ref[:, tile * LANES : (tile + 1) * LANES] = results[:, tile, :].astype(BF16)

    for slot in range(7):
        bias_copy(seq, slot, seq).wait_send()
    for d in range(1, 8):
        share(means, mean_send, mean_recv, d).wait_send()
        share(sums, sum_send, sum_recv, d).wait_send()
    for side, source in enumerate((y, y, y, core)):
        own_copy(side, source).wait_send()
    for group in range(GROUPS):
        for d in (1, 2, 3):
            z_copy(group, d).wait_send()
        for side in range(3):
            y_copy(group, side, y).wait_send()
        for slot in range(4):
            core_copy(group, slot, y, core).wait_send()


def on_device(
    extra_activations,
    twofold_representation,
    present_indicator,
    amino_presence,
    twofold_offset_matrix,
    horizontal_matrix,
    horizontal_exit_matrix,
    vertical_matrix,
    vertical_exit_matrix,
):
    operands = [
        extra_activations,
        twofold_representation,
        present_indicator,
        amino_presence.reshape(1, RES),
        twofold_offset_matrix.T,
        horizontal_matrix,
        horizontal_exit_matrix,
        vertical_matrix,
        vertical_exit_matrix,
    ]
    dma, vmem = pltpu.SemaphoreType.DMA, pltpu.VMEM
    return pl.pallas_call(
        fused_kernel,
        out_shape=jax.ShapeDtypeStruct((SEQS, RES * 64), BF16),
        in_specs=[pl.BlockSpec(memory_space=pltpu.HBM)] * len(operands),
        out_specs=pl.BlockSpec(memory_space=vmem),
        scratch_shapes=[vmem(operand.shape, operand.dtype) for operand in operands]
        + [
            vmem((4, 4, 2, ROWS, LANES), BF16),
            vmem((8, 272, LANES), BF16),
            vmem((SEQS, PAIRS, LANES), F32),
            vmem((256, LANES), F32),
            vmem((512, 512), F32),
            vmem((SEQS, 512, LANES), BF16),
            vmem((SEQS, 32, LANES), F32),
            vmem((SEQS, 32, LANES), BF16),
            vmem((512, 512), F32),
            vmem((512, 512), F32),
            vmem((256, LANES), F32),
            vmem((256, LANES), F32),
            vmem((256, LANES), BF16),
            vmem((256, LANES), BF16),
            vmem((256, LANES), F32),
            vmem((256, LANES), F32),
            vmem((SEQS, PAIRS, LANES), F32),
            vmem((SEQS, PAIRS, LANES), F32),
            vmem((8, PAIRS, LANES), BF16),
            vmem((8, 32, LANES), BF16),
            dma((len(operands),)),
            dma((GROUPS, 10)),
            dma((4,)),
            dma((4,)),
            dma((4, GROUPS)),
            dma((3, GROUPS)),
            dma((4, GROUPS)),
            dma((7,)),
            dma((8,)),
            dma((8,)),
            dma((8,)),
            dma((8,)),
            dma((8,)),
        ],
        compiler_params=pltpu.CompilerParams(
            collective_id=0, has_side_effects=True, vmem_limit_bytes=60 << 20
        ),
        name="fused",
    )(*operands)


def solution(mesh):
    in_specs = (
        P("seq", "res"),
        P("res", "seq", None),
        P("seq", "res"),
        P("res"),
        P(),
        P(),
        P(),
        P(),
        P(),
    )
    out_specs = P("seq", "res")
    return jax.shard_map(
        on_device, mesh=mesh, in_specs=in_specs, out_specs=out_specs, check_vma=False
    )
```
